32 devices in a mesh: group: 2 (over x), ctx: 8 (over z, y), head: 2 (over core).
Axes of the slice: x: 2, y: 2, z: 4, core: 2. Of those that a mesh axis runs over, the one named last changes fastest.
Arguments:
- x_in: bfloat16 [8192, 4096], P(('group', 'ctx'), 'head'), parts along dimension 0, may hold values from -0.625 to 0.625
- b_in: bfloat16 [8192, 128], P(('group', 'ctx')), parts along dimension 0, may hold values from -0.5 to 0.5
- c_in: bfloat16 [8192, 128], P(('group', 'ctx')), parts along dimension 0, may hold values from -0.5 to 0.5
- loga: float32 [8192, 64], P(('group', 'ctx'), 'head'), parts along dimension 0, may hold values from -0.8 to 0, as said below
- dout: bfloat16 [8192, 2048], P(('group', 'ctx')), parts along dimension 0, may hold values from -0.09375 to 0.09375
- w_out: bfloat16 [2048, 4096], P(None, 'head'), may hold values from -0.09375 to 0.09375
Outputs:
- grad_x: bfloat16 [8192, 4096], P(('group', 'ctx'), 'head'), parts along dimension 0
- grad_b: float32 [8192, 128], P(('group', 'ctx')), parts along dimension 0
- grad_c: float32 [8192, 128], P(('group', 'ctx')), parts along dimension 0
- grad_loga: float32 [8192, 64], P(('group', 'ctx'), 'head'), parts along dimension 0
- weight_grad: float32 [4096, 4096], P(('group', 'ctx'), 'head'), parts along dimension 0
The draws below stay inside these ranges and needn't reach their ends.
There are 2 independent parts, one for each index of `group`. The reference program is written for one: setup_inputs(seed, part) draws one part's arguments, and reference() takes and returns one part's arrays. A program takes and returns all parts, laid end to end along the dimension named above; an argument that names none is the same for every part. Nothing has to cross between parts.
Inputs may be any that keep to these rules, and one draw needn't show every extreme that they name: `loga`: log decays of each step and head; negative.
All inputs are finite; a program needn't handle non-finite values.
Results may differ from the reference program's by a relative error of at most 0.017.
Values may be sent and summed in bfloat16 or wider, within the bound.
No kernel may reach another device: no remote copies, remote signals or barrier semaphores. Data moves between devices by JAX's collectives and lax.ppermute only.
A program may use at most 128 MiB of HBM per device.

```python
import math
import jax
import jax.numpy as jnp
from jax import lax

DM = 2048
RECURRENT_GROUPS = 64
STATE = 128
STRETCH = 256
TOK_DEV = 512
INNER = 4096
STEPS = 4096
N_CTX = 8


def draw_loga(key, part):
    sampler_seeds = jax.random.split(jax.random.fold_in(key, 17), 7)
    slow_share = 0.5
    slow_pick = jax.random.uniform(sampler_seeds[0], (RECURRENT_GROUPS,), jnp.float32) < slow_share
    slower_rate = jnp.exp(jax.random.uniform(sampler_seeds[1], (RECURRENT_GROUPS,), jnp.float32, math.log(1e-06), math.log(1e-05)))
    fast_rate = jnp.exp(jax.random.uniform(sampler_seeds[2], (RECURRENT_GROUPS,), jnp.float32, math.log(0.02), math.log(0.035)))
    rate = jnp.where(slow_pick, slower_rate, fast_rate)
    blocks = STEPS // STRETCH
    block_factor = jnp.exp(jax.random.uniform(sampler_seeds[3], (blocks, 1, RECURRENT_GROUPS), jnp.float32, math.log(0.5), math.log(2.0)))
    jitter = jax.random.uniform(sampler_seeds[4], (blocks, STRETCH, RECURRENT_GROUPS), jnp.float32, 0.5, 1.5)
    entry_lines = -(rate[None, None, :] * block_factor * jitter).reshape(STEPS, RECURRENT_GROUPS)
    position_number = jax.random.randint(sampler_seeds[5], (2,), 0, STEPS)
    segment_lengths = jnp.log(jax.random.uniform(sampler_seeds[6], (2, RECURRENT_GROUPS), jnp.float32, 0.5, 0.8))
    entry_lines = entry_lines.at[position_number].add(segment_lengths)
    return entry_lines.astype(jnp.float32)


def levels(stream_key, dims, cuts, low, top_value):
    def one(axis_at, shards_of):
        steps = jax.random.uniform(jax.random.fold_in(jax.random.fold_in(stream_key, 6), axis_at), (shards_of,), jnp.float32, low / len(cuts), top_value / len(cuts))
        return jnp.repeat(jnp.exp(steps), dims[axis_at] // shards_of).reshape((-1,) + (1,) * (len(dims) - axis_at - 1))

    loudness = one(*cuts[0])
    for cut in cuts[1:]:
        loudness = loudness * one(*cut)
    return loudness


def centred(stream_key, extent, scale, limit, cuts=(), held_as=jnp.bfloat16):
    level = levels(stream_key, extent, cuts, -0.22, 0.18) if cuts else 1.0
    result = jax.random.normal(stream_key, extent, jnp.float32) * scale * level
    return jnp.minimum(jnp.maximum(result, -limit), limit).astype(held_as)


def setup_inputs(seed: int = 0, part: int = 0) -> dict:
    key_of = jax.random.split(jax.random.key(seed), 7)
    own_keys = jax.random.split(jax.random.fold_in(key_of[6], part), 7)
    return {
        "x_in": centred(own_keys[0], (STEPS, INNER), 0.1, 0.625, ((0, 8), (1, 2))),
        "b_in": centred(own_keys[1], (STEPS, STATE), STATE ** -0.5, 0.5, ((0, 8),)),
        "c_in": centred(own_keys[2], (STEPS, STATE), STATE ** -0.5, 0.5, ((0, 8),)),
        "loga": draw_loga(jax.random.fold_in(jax.random.fold_in(key_of[6], part), 71), part),
        "dout": centred(own_keys[4], (STEPS, DM), (STEPS ** -0.5), 0.09375, ((0, 8),)),
        "w_out": centred(key_of[5], (DM, INNER), INNER ** -0.5, 0.09375, ((1, 2),)),
    }


masked_out = -1e+30
highest = lax.Precision.HIGHEST

def block_forward(state, x_block, input_matrix_tile, c_block, l_block):
    cum = jnp.cumsum(l_block, axis=0)
    count = x_block.shape[0]
    order = jnp.arange(count)
    lower = order[:, None] >= order[None, :]
    cum_t = cum.T
    diff = cum_t[:, :, None] - cum_t[:, None, :]
    decay = jnp.exp(jnp.where(lower[None, :, :], diff, masked_out))
    scores = jnp.dot(c_block, input_matrix_tile.T, precision=highest)
    weights = decay * scores[None, :, :]
    inside = jnp.einsum('hij,jhp->ihp', weights, x_block, precision=highest)
    lead = jnp.exp(cum)
    carried = jnp.einsum('in,nhp->ihp', c_block, state, precision=highest) * lead[:, :, None]
    tail = jnp.exp(cum[-1][None, :] - cum)
    fresh = jnp.einsum('jn,jhp->nhp', input_matrix_tile, x_block * tail[:, :, None], precision=highest)
    next_state = state * jnp.exp(cum[-1])[None, :, None] + fresh
    return (next_state, inside + carried)

def local_forward(x_value, b_value, c_value, l_value, start_state):
    row_count, head_count, head_width = x_value.shape
    blocks = row_count // STRETCH
    x_blocks = x_value.reshape(blocks, STRETCH, head_count, head_width)
    b_blocks = b_value.reshape(blocks, STRETCH, b_value.shape[1])
    c_blocks = c_value.reshape(blocks, STRETCH, c_value.shape[1])
    l_blocks = l_value.reshape(blocks, STRETCH, head_count)
    stepper = jax.checkpoint(block_forward)

    def advance(state, pieces):
        return stepper(state, pieces[0], pieces[1], pieces[2], pieces[3])
    final, outputs = lax.scan(advance, start_state, (x_blocks, b_blocks, c_blocks, l_blocks))
    return (outputs.reshape(row_count, head_count, head_width), final)

def reference(x_in, b_in, c_in, loga, dout, w_out):
    step_count, width = x_in.shape
    head_count = loga.shape[1]
    head_width = width // head_count
    state_count = b_in.shape[1]
    x_float = x_in.astype(jnp.float32).reshape(step_count, head_count, head_width)
    b_float = b_in.astype(jnp.float32)
    c_float = c_in.astype(jnp.float32)
    grad_y = jnp.dot(dout, w_out, preferred_element_type=jnp.float32).reshape(step_count, head_count, head_width)
    start_state = jnp.zeros((state_count, head_count, head_width), jnp.float32)

    def forward_only(x_value, b_value, c_value, l_value):
        return local_forward(x_value, b_value, c_value, l_value, start_state)[0]
    ssm_y, pull = jax.vjp(forward_only, x_float, b_float, c_float, loga)
    grad_x32, grad_b, grad_c, grad_loga = pull(grad_y)
    y_half = ssm_y.reshape(step_count, width).astype(jnp.bfloat16)
    d_blocks = dout.reshape(N_CTX, TOK_DEV, dout.shape[1])
    y_blocks = y_half.reshape(N_CTX, TOK_DEV, width)

    def accumulate(total, pair):
        part = lax.dot_general(pair[0], pair[1], (((0,), (0,)), ((), ())), preferred_element_type=jnp.float32)
        quantized_result = lax.optimization_barrier(part.astype(jnp.bfloat16))
        return (total + quantized_result.astype(jnp.float32), None)
    weight_grad, _ = lax.scan(accumulate, jnp.zeros((dout.shape[1], width), jnp.float32), (d_blocks, y_blocks))
    grad_x = grad_x32.reshape(step_count, width).astype(jnp.bfloat16)
    return (grad_x, grad_b, grad_c, grad_loga, weight_grad)
```

```python
import functools
import math

import jax
import jax.numpy as jnp
from jax import lax
from jax.experimental import pallas as pl
from jax.experimental.pallas import tpu as pltpu
from jax.sharding import PartitionSpec as P

BLOCK = 128
LANES = 128
GROUP_HEADS = 8
LOG2E = math.log2(math.e)
F32 = jnp.float32
BF16 = jnp.bfloat16
EXACT = lax.Precision.HIGHEST
NT = (((1,), (1,)), ((), ()))
TN = (((0,), (0,)), ((), ()))
MIB = 2**20


def dot(a, b, dims=(((1,), (0,)), ((), ())), precision=None):
    return lax.dot_general(a, b, dims, precision=precision, preferred_element_type=F32)


def low_lanes(rows):
    return lax.broadcasted_iota(jnp.int32, (rows, LANES), 1) < LANES // 2


def pair_columns(small, pair):
    rows = small.shape[0]
    even = jnp.broadcast_to(small[:, 2 * pair : 2 * pair + 1], (rows, LANES))
    odd = jnp.broadcast_to(small[:, 2 * pair + 1 : 2 * pair + 2], (rows, LANES))
    return jnp.where(low_lanes(rows), even, odd)


def transposed(x):
    return x.astype(F32).T.astype(BF16)


def start_kernel(q_ref, loga_ref, x_ref, b_ref, cum_ref, cumt_ref, lead_ref, send_ref, keep_ref, tot_ref, own):
    rows, heads = loga_ref.shape
    width = x_ref.shape[1]
    half = width // 2
    states = b_ref.shape[1]
    r = lax.broadcasted_iota(jnp.int32, (BLOCK, BLOCK), 0)
    c = lax.broadcasted_iota(jnp.int32, (BLOCK, BLOCK), 1)
    tri = (r >= c).astype(F32)
    eye = (
        lax.broadcasted_iota(jnp.int32, (heads, heads), 0)
        == lax.broadcasted_iota(jnp.int32, (heads, heads), 1)
    ).astype(F32)
    base = jnp.zeros((1, heads), F32)
    whole = []
    for k in range(rows // BLOCK):
        at = slice(k * BLOCK, (k + 1) * BLOCK)
        cum = dot(tri, loga_ref[at, :] * LOG2E, precision=EXACT)
        for g in range(heads // GROUP_HEADS):
            hs = slice(g * GROUP_HEADS, (g + 1) * GROUP_HEADS)
            cum_ref[g, at, :] = cum[:, hs]
        cumt_ref[:, at] = dot(eye, cum, NT, precision=EXACT)
        whole.append(cum + base)
        base = base + cum[BLOCK - 1 :, :]
    for k, cum in enumerate(whole):
        at = slice(k * BLOCK, (k + 1) * BLOCK)
        lead = jnp.exp2(cum)
        for g in range(heads // GROUP_HEADS):
            hs = slice(g * GROUP_HEADS, (g + 1) * GROUP_HEADS)
            lead_ref[g, at, :] = lead[:, hs]
    tails = [jnp.exp2(base - cum) for cum in whole]
    b_t = transposed(b_ref[...])
    total = jnp.broadcast_to(base, (8, heads))
    for p in range(heads // 2):
        ps = slice(p * LANES, (p + 1) * LANES)
        xs = jnp.concatenate(
            [
                (x_ref[k * BLOCK : (k + 1) * BLOCK, ps].astype(F32) * pair_columns(t, p)).astype(BF16)
                for k, t in enumerate(tails)
            ],
            axis=0,
        )
        own[0:states, ps] = dot(b_t, xs)
        own[states : states + 8, ps] = pair_columns(total, p)
    q = q_ref[0]
    mine = pl.ds(pl.multiple_of(q * half, LANES), half)
    other = pl.ds(pl.multiple_of((1 - q) * half, LANES), half)
    keep_ref[...] = own[0:states, mine]
    tot_ref[...] = own[states : states + 8, mine]
    send_ref[0:states, :] = own[0:states, other].astype(BF16)
    t = own[states : states + 8, other]
    hi = t.astype(BF16)
    mid = (t - hi.astype(F32)).astype(BF16)
    lo = (t - hi.astype(F32) - mid.astype(F32)).astype(BF16)
    row = lax.broadcasted_iota(jnp.int32, (8, half), 0)
    pieces = jnp.where(
        row == 0, hi.astype(F32), jnp.where(row == 1, mid.astype(F32), jnp.where(row == 2, lo.astype(F32), 0.0))
    )
    send_ref[states : states + 16, :] = jnp.concatenate([pieces, jnp.zeros_like(pieces)], axis=0).astype(BF16)


def start(q, loga, x, b):
    rows, heads = loga.shape
    width = x.shape[1]
    states = b.shape[1]
    groups = heads // GROUP_HEADS
    vmem = pl.BlockSpec(memory_space=pltpu.VMEM)
    return pl.pallas_call(
        start_kernel,
        in_specs=[pl.BlockSpec(memory_space=pltpu.SMEM), vmem, vmem, vmem],
        out_specs=[vmem] * 6,
        out_shape=[
            jax.ShapeDtypeStruct((groups, rows, GROUP_HEADS), F32),
            jax.ShapeDtypeStruct((heads, rows), F32),
            jax.ShapeDtypeStruct((groups, rows, GROUP_HEADS), F32),
            jax.ShapeDtypeStruct((states + 16, width // 2), BF16),
            jax.ShapeDtypeStruct((states, width // 2), F32),
            jax.ShapeDtypeStruct((8, width // 2), F32),
        ],
        scratch_shapes=[pltpu.VMEM((states + 8, width), F32)],
        compiler_params=pltpu.CompilerParams(vmem_limit_bytes=24 * MIB),
        cost_estimate=pl.CostEstimate(flops=10**9, bytes_accessed=6 * MIB, transcendentals=10**5),
        name="start",
    )(q, loga, x, b)


def block_diagonal(pair):
    low = low_lanes(pair.shape[0])
    wide = pair.astype(F32)
    zero = jnp.zeros_like(wide)
    return jnp.concatenate([jnp.where(low, wide, zero), jnp.where(low, zero, wide)], axis=0).astype(BF16)


def forward_kernel(x_ref, b_ref, c_ref, cum_ref, cumt_ref, y_ref, scores):
    rows = x_ref.shape[0]
    blocks = rows // BLOCK

    @pl.when(pl.program_id(0) == 0)
    def _():
        r = lax.broadcasted_iota(jnp.int32, (BLOCK, BLOCK), 0)
        c = lax.broadcasted_iota(jnp.int32, (BLOCK, BLOCK), 1)
        for k in range(blocks):
            at = slice(k * BLOCK, (k + 1) * BLOCK)
            scores[k] = jnp.where(r >= c, dot(c_ref[at, :], b_ref[at, :], NT), 0.0)

    low = low_lanes(BLOCK)
    b_t = [transposed(b_ref[k * BLOCK : (k + 1) * BLOCK, :]) for k in range(blocks)]
    for p in range(GROUP_HEADS // 2):
        ps = slice(p * LANES, (p + 1) * LANES)
        state = None
        for k in range(blocks):
            at = slice(k * BLOCK, (k + 1) * BLOCK)
            a0 = jnp.broadcast_to(cum_ref[0, at, 2 * p : 2 * p + 1], (BLOCK, LANES))
            a1 = jnp.broadcast_to(cum_ref[0, at, 2 * p + 1 : 2 * p + 2], (BLOCK, LANES))
            r0 = cumt_ref[2 * p : 2 * p + 1, at]
            r1 = cumt_ref[2 * p + 1 : 2 * p + 2, at]
            s = scores[k]
            w0 = jnp.exp2(jnp.minimum(a0 - r0, 0.0)) * s
            w1 = jnp.exp2(jnp.minimum(a1 - r1, 0.0)) * s
            x = x_ref[at, ps]
            y = dot(jnp.concatenate([w0, w1], axis=1).astype(BF16), block_diagonal(x))
            both = jnp.where(low, a0, a1)
            if k > 0:
                y = y + jnp.exp2(both) * dot(c_ref[at, :], state.astype(BF16))
            if k < blocks - 1:
                last = both[BLOCK - 1 :, :]
                fresh = dot(b_t[k], (x.astype(F32) * jnp.exp2(last - both)).astype(BF16))
                state = fresh if k == 0 else jnp.exp2(last) * state + fresh
            y_ref[at, ps] = y


def forward(x, b, c, cum, cumt):
    rows, width = x.shape
    groups = cum.shape[0]
    wide = width // groups
    return pl.pallas_call(
        forward_kernel,
        grid=(groups,),
        in_specs=[
            pl.BlockSpec((rows, wide), lambda g: (0, g)),
            pl.BlockSpec(b.shape, lambda g: (0, 0)),
            pl.BlockSpec(c.shape, lambda g: (0, 0)),
            pl.BlockSpec((1, rows, GROUP_HEADS), lambda g: (g, 0, 0)),
            pl.BlockSpec((GROUP_HEADS, rows), lambda g: (g, 0)),
        ],
        out_specs=pl.BlockSpec((rows, wide), lambda g: (0, g)),
        out_shape=jax.ShapeDtypeStruct((rows, width), F32),
        scratch_shapes=[pltpu.VMEM((rows // BLOCK, BLOCK, BLOCK), F32)],
        compiler_params=pltpu.CompilerParams(vmem_limit_bytes=24 * MIB),
        cost_estimate=pl.CostEstimate(flops=6 * 10**9, bytes_accessed=7 * MIB, transcendentals=3 * 10**6),
        name="forward",
    )(x, b, c, cum, cumt)


def finish_kernel(y_ref, c_ref, lead_ref, state_ref, out_ref):
    for p in range(GROUP_HEADS // 2):
        ps = slice(p * LANES, (p + 1) * LANES)
        lead = pair_columns(lead_ref[0], p)
        out_ref[:, ps] = (y_ref[:, ps] + lead * dot(c_ref[...], state_ref[:, ps])).astype(BF16)


def finish(y, c, lead, state):
    rows, width = y.shape
    groups = lead.shape[0]
    wide = width // groups
    return pl.pallas_call(
        finish_kernel,
        grid=(groups,),
        in_specs=[
            pl.BlockSpec((rows, wide), lambda g: (0, g)),
            pl.BlockSpec(c.shape, lambda g: (0, 0)),
            pl.BlockSpec((1, rows, GROUP_HEADS), lambda g: (g, 0, 0)),
            pl.BlockSpec((state.shape[0], wide), lambda g: (0, g)),
        ],
        out_specs=pl.BlockSpec((rows, wide), lambda g: (0, g)),
        out_shape=jax.ShapeDtypeStruct((rows, width), BF16),
        compiler_params=pltpu.CompilerParams(vmem_limit_bytes=16 * MIB),
        cost_estimate=pl.CostEstimate(flops=3 * 10**8, bytes_accessed=7 * MIB, transcendentals=0),
        name="finish",
    )(y, c, lead, state)


def adjoint_kernel(dout_ref, w_ref, c_ref, lead_ref, gy_ref, own_ref):
    c_t = transposed(c_ref[...])
    gy = dot(dout_ref[...], w_ref[...])
    gy_ref[...] = gy.astype(BF16)
    for p in range(GROUP_HEADS // 2):
        ps = slice(p * LANES, (p + 1) * LANES)
        scaled = gy[:, ps] * pair_columns(lead_ref[0], p)
        own_ref[:, ps] = dot(c_t, scaled.astype(BF16))


def adjoint(dout, w, c, lead):
    rows, model = dout.shape
    width = w.shape[1]
    groups = lead.shape[0]
    wide = width // groups
    states = c.shape[1]
    return pl.pallas_call(
        adjoint_kernel,
        grid=(groups,),
        in_specs=[
            pl.BlockSpec((rows, model), lambda g: (0, 0)),
            pl.BlockSpec((model, wide), lambda g: (0, g)),
            pl.BlockSpec(c.shape, lambda g: (0, 0)),
            pl.BlockSpec((1, rows, GROUP_HEADS), lambda g: (g, 0, 0)),
        ],
        out_specs=[
            pl.BlockSpec((rows, wide), lambda g: (0, g)),
            pl.BlockSpec((states, wide), lambda g: (0, g)),
        ],
        out_shape=[
            jax.ShapeDtypeStruct((rows, width), BF16),
            jax.ShapeDtypeStruct((states, width), F32),
        ],
        compiler_params=pltpu.CompilerParams(vmem_limit_bytes=24 * MIB),
        cost_estimate=pl.CostEstimate(flops=6 * 10**9, bytes_accessed=14 * MIB, transcendentals=0),
        name="adjoint",
    )(dout, w, c, lead)


def turn_kernel(order_ref, dout_ref, out_ref):
    out_ref[...] = transposed(dout_ref[...])


def turn(order, dout):
    rows, model = dout.shape
    count = order.shape[0]
    tall = model // count
    return pl.pallas_call(
        turn_kernel,
        grid_spec=pltpu.PrefetchScalarGridSpec(
            num_scalar_prefetch=1,
            grid=(count,),
            in_specs=[pl.BlockSpec((rows, tall), lambda i, order: (0, order[i]))],
            out_specs=pl.BlockSpec((tall, rows), lambda i, order: (i, 0)),
        ),
        out_shape=jax.ShapeDtypeStruct((model, rows), BF16),
        compiler_params=pltpu.CompilerParams(vmem_limit_bytes=16 * MIB),
        cost_estimate=pl.CostEstimate(flops=0, bytes_accessed=4 * MIB, transcendentals=0),
        name="turn",
    )(order, dout)


def backward_kernel(
    x_ref, gy_ref, y_ref, b_ref, c_ref, cum_ref, cumt_ref, s_ref, g_ref,
    gx_ref, db_ref, dc_ref, dl_ref,
    scores, dscores,
):
    rows = x_ref.shape[0]
    blocks = rows // BLOCK
    step, steps = pl.program_id(0), pl.num_programs(0)
    r = lax.broadcasted_iota(jnp.int32, (BLOCK, BLOCK), 0)
    c = lax.broadcasted_iota(jnp.int32, (BLOCK, BLOCK), 1)
    upper = r <= c

    @pl.when(step == 0)
    def _():
        for k in range(blocks):
            at = slice(k * BLOCK, (k + 1) * BLOCK)
            scores[k] = jnp.where(upper, dot(b_ref[at, :], c_ref[at, :], NT), 0.0)
        dscores[...] = jnp.zeros_like(dscores)
        db_ref[...] = jnp.zeros_like(db_ref)
        dc_ref[...] = jnp.zeros_like(dc_ref)

    low = low_lanes(BLOCK)
    spots = [slice(k * BLOCK, (k + 1) * BLOCK) for k in range(blocks)]
    b_t = [transposed(b_ref[at, :]) for at in spots]
    c_t = [transposed(c_ref[at, :]) for at in spots]
    sums = [jnp.zeros((GROUP_HEADS, BLOCK), F32)] * blocks
    head_row = lax.broadcasted_iota(jnp.int32, (GROUP_HEADS, LANES), 0)
    head_half = lax.broadcasted_iota(jnp.int32, (GROUP_HEADS, LANES), 1) // (LANES // 2)
    for p in range(GROUP_HEADS // 2):
        ps = slice(p * LANES, (p + 1) * LANES)
        place = (head_row == 2 * p + head_half).astype(BF16)
        columns, tails, entering = [], [], [s_ref[:, ps].astype(F32)]
        for k, at in enumerate(spots):
            a0 = jnp.broadcast_to(cum_ref[0, at, 2 * p : 2 * p + 1], (BLOCK, LANES))
            a1 = jnp.broadcast_to(cum_ref[0, at, 2 * p + 1 : 2 * p + 2], (BLOCK, LANES))
            both = jnp.where(low, a0, a1)
            last = both[BLOCK - 1 :, :]
            columns.append((a0, a1, both, jnp.exp2(last)))
            tail = jnp.exp2(last - both)
            tails.append((tail, (x_ref[at, ps].astype(F32) * tail).astype(BF16)))
            entering.append(jnp.exp2(last) * entering[k] + dot(b_t[k], tails[k][1]))
        g = g_ref[:, ps].astype(F32)
        for k in reversed(range(blocks)):
            at = spots[k]
            a0, a1, both, span = columns[k]
            tail, xs = tails[k]
            d0 = jnp.exp2(jnp.minimum(cumt_ref[2 * p : 2 * p + 1, at] - a0, 0.0))
            d1 = jnp.exp2(jnp.minimum(cumt_ref[2 * p + 1 : 2 * p + 2, at] - a1, 0.0))
            s = scores[k]
            x, gy = x_ref[at, ps], gy_ref[at, ps]
            g_half = g.astype(BF16)
            weights = jnp.concatenate([d0 * s, d1 * s], axis=1).astype(BF16)
            gx = dot(weights, block_diagonal(gy)) + tail * dot(b_ref[at, :], g_half)
            gx_ref[at, ps] = gx.astype(BF16)
            dw = dot(block_diagonal(x), gy, NT)
            dscores[k] += d0 * dw[:BLOCK] + d1 * dw[BLOCK:]
            db_ref[at, :] += dot(xs, g_half, NT)
            gys = (gy.astype(F32) * jnp.exp2(both)).astype(BF16)
            dc_ref[at, :] += dot(gys, entering[k].astype(BF16), NT)
            term = gy.astype(F32) * y_ref[at, ps].astype(F32) - x.astype(F32) * gx
            end = jnp.sum(entering[k + 1] * g, axis=0, keepdims=True)
            term = term + jnp.where(r == BLOCK - 1, end, 0.0)
            hi = term.astype(BF16)
            lo = (term - hi.astype(F32)).astype(BF16)
            sums[k] = sums[k] + dot(place, hi, NT) + dot(place, lo, NT)
            g = span * g + dot(c_t[k], gys)
    for k, at in enumerate(spots):
        dl_ref[:, at] = dot(sums[k], (r >= c).astype(F32), precision=EXACT)

    @pl.when(step == steps - 1)
    def _():
        for k, at in enumerate(spots):
            ds = jnp.where(upper, dscores[k], 0.0)
            db_ref[at, :] += dot(ds.astype(BF16), c_ref[at, :])
            dc_ref[at, :] += dot(ds.T.astype(BF16), b_ref[at, :])


def backward(x, gy, y, b, c, cum, cumt, entering, leaving):
    rows, width = x.shape
    groups = cum.shape[0]
    heads = groups * GROUP_HEADS
    wide = width // groups
    states = b.shape[1]
    tall = pl.BlockSpec((rows, wide), lambda g: (0, g))
    whole = pl.BlockSpec((rows, states), lambda g: (0, 0))
    state = pl.BlockSpec((states, wide), lambda g: (0, g))
    return pl.pallas_call(
        backward_kernel,
        grid=(groups,),
        in_specs=[
            tall, tall, tall, whole, whole,
            pl.BlockSpec((1, rows, GROUP_HEADS), lambda g: (g, 0, 0)),
            pl.BlockSpec((GROUP_HEADS, rows), lambda g: (g, 0)),
            state, state,
        ],
        out_specs=[tall, whole, whole, pl.BlockSpec((GROUP_HEADS, rows), lambda g: (g, 0))],
        out_shape=[
            jax.ShapeDtypeStruct((rows, width), BF16),
            jax.ShapeDtypeStruct((rows, states), F32),
            jax.ShapeDtypeStruct((rows, states), F32),
            jax.ShapeDtypeStruct((heads, rows), F32),
        ],
        scratch_shapes=[pltpu.VMEM((rows // BLOCK, BLOCK, BLOCK), F32)] * 2,
        compiler_params=pltpu.CompilerParams(vmem_limit_bytes=24 * MIB),
        cost_estimate=pl.CostEstimate(flops=10**10, bytes_accessed=10 * MIB, transcendentals=3 * 10**6),
        name="backward",
    )(x, gy, y, b, c, cum, cumt, entering, leaving)


def ring_order(count):
    if count == 8:
        return [0, 2, 4, 6, 7, 5, 3, 1]
    return list(range(count))


def scan_states(keep, recv, my_total, other_total, first, up):
    count = lax.axis_size("ctx")
    by = 2 if up else -2
    pairs = [(i, i + by) for i in range(count) if 0 <= i + by < count]
    mine, others = jnp.exp2(my_total), jnp.exp2(other_total)
    recv = recv.astype(F32)
    both = jnp.where(first, others * keep + recv, mine * recv + keep)
    span = jnp.exp2(my_total + other_total)
    out = both
    for hop in range(count // 2 - 1):
        enter = lax.ppermute(out.astype(BF16), "ctx", pairs).astype(F32)
        if hop < count // 2 - 2:
            out = span * enter + both
    after_me, after_other = mine * enter + keep, others * enter + recv
    own = jnp.where(first, enter, after_other)
    partners = jnp.where(first, after_me, enter)
    return own.astype(BF16), partners.astype(BF16)


def on_device(x, b, c, loga, dout, w):
    count = lax.axis_size("ctx")
    me = lax.axis_index("ctx")
    q = lax.rem(me, 2)
    width = x.shape[1]
    half = width // 2
    states = b.shape[1]
    swap = [(i, i ^ 1) for i in range(count)]
    cum, cumt, lead, send, keep, total = start(q.reshape(1), loga, x, b)
    my_total = total[0:1]
    got = lax.ppermute(send, "ctx", swap)
    pieces = got[states : states + 3].astype(F32)
    other_total = pieces[0:1] + pieces[1:2] + pieces[2:3]
    own, partners = scan_states(keep, got[:states], my_total, other_total, q == 0, True)
    back = lax.ppermute(partners, "ctx", swap)
    entering = jnp.concatenate([jnp.where(q == 0, own, back), jnp.where(q == 0, back, own)], axis=1)

    y_local = forward(x, b, c, cum, cumt)
    gy, adj = adjoint(dout, w, c, lead)
    adj_keep = jnp.where(q == 0, adj[:, :half], adj[:, half:])
    adj_send = jnp.where(q == 0, adj[:, half:], adj[:, :half]).astype(BF16)
    adj_got = lax.ppermute(adj_send, "ctx", swap)
    own_g, partners_g = scan_states(adj_keep, adj_got, my_total, other_total, q == 1, False)
    back_g = lax.ppermute(partners_g, "ctx", swap)
    leaving = jnp.concatenate([jnp.where(q == 0, own_g, back_g), jnp.where(q == 0, back_g, own_g)], axis=1)

    ring = ring_order(count)
    places = [ring.index(i) for i in range(count)]
    at = jnp.asarray(places, jnp.int32)[me]
    order = jnp.asarray(ring, jnp.int32)[lax.rem(at + jnp.arange(count, dtype=jnp.int32), count)]
    dout_t = turn(order, dout)
    tall = dout.shape[1] // count

    y_half = finish(y_local, c, lead, entering)
    flows = []
    for f, by in enumerate((1, -1)):
        hops = [(ring[i], ring[(i + by) % count]) for i in range(count)]
        flows.append([hops, by, slice(f * half, (f + 1) * half), None])
    for step in range(count):
        for flow in flows:
            hops, by, cols, got_sum = flow
            offset = (by * (count - 1 - step)) % count
            part = dot(dout_t[offset * tall : (offset + 1) * tall], y_half[:, cols])
            if got_sum is not None:
                part = part + got_sum.astype(F32)
            flow[3] = part if step == count - 1 else lax.ppermute(part.astype(BF16), "ctx", hops)
    weight_grad = jnp.concatenate([flow[3] for flow in flows], axis=1)

    grad_x, db, dc, dl = backward(x, gy, y_half, b, c, cum, cumt, entering, leaving)
    terms = jnp.concatenate([db, dc], axis=0).astype(BF16)
    summed = terms.astype(F32) + lax.ppermute(terms, "head", [(0, 1), (1, 0)]).astype(F32)
    rows = x.shape[0]
    return grad_x, summed[:rows], summed[rows:], dl.T, weight_grad


def solution(mesh):
    tokens = ("group", "ctx")
    placed = (
        P(tokens, "head"),
        P(tokens, None),
        P(tokens, None),
        P(tokens, "head"),
        P(tokens, None),
        P(None, "head"),
    )
    return jax.shard_map(
        on_device,
        mesh=mesh,
        in_specs=placed,
        out_specs=(
            P(tokens, "head"),
            P(tokens, None),
            P(tokens, None),
            P(tokens, "head"),
            P(tokens, "head"),
        ),
        check_vma=False,
    )
```

```python
import functools
import math

import jax
import jax.numpy as jnp
from jax import lax
from jax.experimental import pallas as pl
from jax.experimental.pallas import tpu as pltpu
from jax.sharding import PartitionSpec as P

BLOCK = 128
LANES = 128
GROUP_HEADS = 8
LOG2E = math.log2(math.e)
F32 = jnp.float32
BF16 = jnp.bfloat16
EXACT = lax.Precision.HIGHEST
NT = (((1,), (1,)), ((), ()))
TN = (((0,), (0,)), ((), ()))
MIB = 2**20


def dot(a, b, dims=(((1,), (0,)), ((), ())), precision=None):
    return lax.dot_general(a, b, dims, precision=precision, preferred_element_type=F32)


def low_lanes(rows):
    return lax.broadcasted_iota(jnp.int32, (rows, LANES), 1) < LANES // 2


def pair_columns(small, pair):
    rows = small.shape[0]
    even = jnp.broadcast_to(small[:, 2 * pair : 2 * pair + 1], (rows, LANES))
    odd = jnp.broadcast_to(small[:, 2 * pair + 1 : 2 * pair + 2], (rows, LANES))
    return jnp.where(low_lanes(rows), even, odd)


def transposed(x):
    return x.astype(F32).T.astype(BF16)


def place_in_pair():
    return lax.rem(lax.axis_index("ctx"), 2)


def pairs_before(up):
    me, count = lax.axis_index("ctx"), lax.axis_size("ctx")
    return me // 2 if up else (count - 1 - me) // 2


def vmem_ref():
    return pl.BlockSpec(memory_space=pltpu.VMEM)


TOKEN = jax.ShapeDtypeStruct((8, LANES), F32)


def token_ref(grid):
    return pl.BlockSpec((8, LANES), lambda *g: (0, 0)) if grid else vmem_ref()


def give(token):
    token[...] = jnp.zeros_like(token)


def log_rows(t):
    hi = t.astype(BF16).astype(F32)
    mid = (t - hi).astype(BF16).astype(F32)
    lo = t - hi - mid
    row = lax.broadcasted_iota(jnp.int32, t.shape, 0)
    pieces = jnp.where(row == 0, hi, jnp.where(row == 1, mid, jnp.where(row == 2, lo, 0.0)))
    return jnp.concatenate([pieces, jnp.zeros_like(pieces)], axis=0).astype(BF16)


def end_states(x_ref, b_t, tail, total, keep_ref, tot_ref, send_ref, own):
    rows, width = x_ref.shape
    states = b_t.shape[0]
    half = width // 2
    heads = width // (LANES // 2)
    for p in range(heads // 2):
        ps = slice(p * LANES, (p + 1) * LANES)
        xs = (x_ref[:, ps].astype(F32) * pair_columns(tail, p)).astype(BF16)
        own[0:states, ps] = dot(b_t, xs)
        own[states : states + 8, ps] = pair_columns(total, p)
    q = place_in_pair()
    mine = pl.ds(pl.multiple_of(q * half, LANES), half)
    other = pl.ds(pl.multiple_of((1 - q) * half, LANES), half)
    keep_ref[...] = own[0:states, mine]
    tot_ref[...] = own[states : states + 8, mine]
    send_ref[0:states, :] = own[0:states, other].astype(BF16)
    send_ref[states : states + 16, :] = log_rows(own[states : states + 8, other])


def start_kernel(
    loga_ref, x_ref, b_ref, cum_ref, cumt_ref, lead_ref, tail_ref, keep_ref, tot_ref, send_ref, own
):
    heads, rows = loga_ref.shape
    here = x_ref.shape[1] // (LANES // 2)
    r = lax.broadcasted_iota(jnp.int32, (BLOCK, BLOCK), 0)
    c = lax.broadcasted_iota(jnp.int32, (BLOCK, BLOCK), 1)
    base = jnp.zeros((1, heads), F32)
    whole = []
    for k in range(rows // BLOCK):
        at = slice(k * BLOCK, (k + 1) * BLOCK)
        logs = loga_ref[:, at] * LOG2E
        cum = dot((r >= c).astype(F32), logs, NT, precision=EXACT)
        for g in range(heads // GROUP_HEADS):
            cum_ref[g, at, :] = cum[:, g * GROUP_HEADS : (g + 1) * GROUP_HEADS]
        cumt_ref[:, at] = dot(logs, (r <= c).astype(F32), precision=EXACT)
        whole.append(cum + base)
        base = base + cum[BLOCK - 1 :, :]
    whole = jnp.concatenate(whole, axis=0)
    lead, tail = jnp.exp2(whole), jnp.exp2(base - whole)
    for g in range(heads // GROUP_HEADS):
        hs = slice(g * GROUP_HEADS, (g + 1) * GROUP_HEADS)
        lead_ref[g] = lead[:, hs]
    total = jnp.broadcast_to(base, (8, heads))
    for g in range(heads // here):
        hs = slice(g * here, (g + 1) * here)
        tail_ref[g, 0:rows, :] = tail[:, hs]
        tail_ref[g, rows : rows + 8, :] = total[:, hs]
    end_states(x_ref, transposed(b_ref[...]), tail[:, :here], total[:, :here], keep_ref, tot_ref, send_ref, own)


def start(logs, x, b, wide):
    heads, rows = logs.shape
    width = x.shape[1]
    states = b.shape[1]
    groups = heads // GROUP_HEADS
    here = heads * wide // width
    return pl.pallas_call(
        start_kernel,
        grid=(1,),
        in_specs=[
            pl.BlockSpec((heads, rows), lambda i: (0, 0)),
            pl.BlockSpec((rows, wide), lambda i: (0, 0)),
            pl.BlockSpec(b.shape, lambda i: (0, 0)),
        ],
        out_specs=[vmem_ref()] * 7,
        out_shape=[
            jax.ShapeDtypeStruct((groups, rows, GROUP_HEADS), F32),
            jax.ShapeDtypeStruct((heads, rows), F32),
            jax.ShapeDtypeStruct((groups, rows, GROUP_HEADS), F32),
            jax.ShapeDtypeStruct((heads // here, rows + 8, here), F32),
            jax.ShapeDtypeStruct((states, wide // 2), F32),
            jax.ShapeDtypeStruct((8, wide // 2), F32),
            jax.ShapeDtypeStruct((states + 16, wide // 2), BF16),
        ],
        scratch_shapes=[pltpu.VMEM((states + 8, wide), F32)],
        compiler_params=pltpu.CompilerParams(vmem_limit_bytes=12 * MIB),
        cost_estimate=pl.CostEstimate(flops=10**9, bytes_accessed=4 * MIB, transcendentals=10**5),
        name="start",
    )(logs, x, b)


def ends_kernel(x_ref, b_ref, tail_ref, keep_ref, tot_ref, send_ref, own):
    rows = x_ref.shape[0]
    end_states(
        x_ref, transposed(b_ref[...]), tail_ref[0, 0:rows], tail_ref[0, rows : rows + 8], keep_ref, tot_ref, send_ref, own
    )


def ends(x, b, tail, group, wide):
    rows = x.shape[0]
    states = b.shape[1]
    return pl.pallas_call(
        ends_kernel,
        grid=(1,),
        in_specs=[
            pl.BlockSpec((rows, wide), lambda i: (0, group)),
            pl.BlockSpec(b.shape, lambda i: (0, 0)),
            pl.BlockSpec((1, *tail.shape[1:]), lambda i: (group, 0, 0)),
        ],
        out_specs=[vmem_ref()] * 3,
        out_shape=[
            jax.ShapeDtypeStruct((states, wide // 2), F32),
            jax.ShapeDtypeStruct((8, wide // 2), F32),
            jax.ShapeDtypeStruct((states + 16, wide // 2), BF16),
        ],
        scratch_shapes=[pltpu.VMEM((states + 8, wide), F32)],
        compiler_params=pltpu.CompilerParams(vmem_limit_bytes=8 * MIB),
        cost_estimate=pl.CostEstimate(flops=10**9, bytes_accessed=3 * MIB, transcendentals=0),
        name="ends",
    )(x, b, tail)


def joined_kernel(keep_ref, got_ref, tot_ref, other_ref, *refs, first_is, from_message):
    out_ref, both_ref, other_out = refs[-3:]
    states = keep_ref.shape[0]
    got = got_ref[0:states, :].astype(F32)
    if from_message:
        pieces = got_ref[states : states + 16, :].astype(F32)
        other = pieces[0:1] + pieces[1:2] + pieces[2:3]
    else:
        other = other_ref[0:1, :]
    mine = tot_ref[0:1, :]
    first = place_in_pair() == first_is
    later = jnp.exp2(jnp.where(first, other, mine))
    keep = keep_ref[...]
    both = jnp.where(first, later * keep + got, later * got + keep)
    both_ref[...] = both
    out_ref[0:states, :] = both.astype(BF16)
    out_ref[states : states + 16, :] = log_rows(jnp.broadcast_to(mine + other, (8, keep.shape[1])))
    other_out[...] = jnp.broadcast_to(other, other_out.shape)


def small_kernel(body, name, shapes, arrays, after):
    return pl.pallas_call(
        body,
        in_specs=[vmem_ref()] * (len(arrays) + len(after)),
        out_specs=[vmem_ref()] * len(shapes),
        out_shape=[jax.ShapeDtypeStruct(*s) for s in shapes],
        compiler_params=pltpu.CompilerParams(vmem_limit_bytes=4 * MIB),
        cost_estimate=pl.CostEstimate(flops=10**6, bytes_accessed=MIB, transcendentals=0),
        name=name,
    )(*arrays, *after)


def joined(keep, got, tot, other, up, after):
    states, half = keep.shape
    body = functools.partial(joined_kernel, first_is=0 if up else 1, from_message=other is None)
    shapes = [((states + 16, half), BF16), ((states, half), F32), ((8, half), F32)]
    return small_kernel(body, "joined", shapes, (keep, got, tot, tot if other is None else other), after)


def carry_kernel(both_ref, in_ref, tot_ref, other_ref, *refs, up):
    out_ref = refs[-1]
    states = both_ref.shape[0]
    seen = (pairs_before(up) > 0).astype(F32)
    span = jnp.exp2(tot_ref[0:1, :] + other_ref[0:1, :]) * seen
    out_ref[...] = (both_ref[...] + span * in_ref[0:states, :].astype(F32)).astype(BF16)


def carry(both, into, tot, other, up, after):
    body = functools.partial(carry_kernel, up=up)
    return small_kernel(body, "carry", [(both.shape, BF16)], (both, into, tot, other), after)[0]


def entered_kernel(keep_ref, got_ref, tot_ref, other_ref, near_ref, *refs, up, far):
    own_ref, partner_ref = refs[-2:]
    states = keep_ref.shape[0]
    enter = near_ref[0:states, :].astype(F32)
    if far:
        pieces = near_ref[states : states + 16, :].astype(F32)
        span = jnp.exp2(pieces[0:1] + pieces[1:2] + pieces[2:3])
        enter = enter + jnp.where(pairs_before(up) > 1, span * refs[0][...].astype(F32), 0.0)
    enter = jnp.where(pairs_before(up) > 0, enter, 0.0)
    mine, other = jnp.exp2(tot_ref[0:1, :]), jnp.exp2(other_ref[0:1, :])
    first = place_in_pair() == (0 if up else 1)
    after_me = mine * enter + keep_ref[...]
    after_other = other * enter + got_ref[0:states, :].astype(F32)
    own_ref[...] = jnp.where(first, enter, after_other).astype(BF16)
    partner_ref[...] = jnp.where(first, after_me, enter).astype(BF16)


def entered(keep, got, tot, other, near, far, up, after):
    body = functools.partial(entered_kernel, up=up, far=far is not None)
    shapes = [(keep.shape, BF16)] * 2
    arrays = (keep, got, tot, other, near) + (() if far is None else (far,))
    return small_kernel(body, "entered", shapes, arrays, after)


def scan(send, keep, tot, other, up, afters):
    count = lax.axis_size("ctx")
    swap = [(i, i ^ 1) for i in range(count)]

    def hop(x, by):
        by = 2 * by if up else -2 * by
        return lax.ppermute(x, "ctx", [(i, (i + by) % count) for i in range(count) if up or 0 <= i + by < count])

    got = lax.ppermute(send, "ctx", swap)
    message, both, other = joined(keep, got, tot, other, up, afters[0])
    near = hop(message, 1)
    if count == 8:
        far = hop(carry(both, near, tot, other, up, afters[1]), 2)
    else:
        far = None
        for _ in range(count // 2 - 2):
            near = hop(carry(both, near, tot, other, up, afters[1]), 1)
    own, partners = entered(keep, got, tot, other, near, far, up, afters[2])
    return own, lax.ppermute(partners, "ctx", swap), other


def block_diagonal(pair):
    low = low_lanes(pair.shape[0])
    wide = pair.astype(F32)
    zero = jnp.zeros_like(wide)
    return jnp.concatenate([jnp.where(low, wide, zero), jnp.where(low, zero, wide)], axis=0).astype(BF16)


def forward_kernel(x_ref, b_ref, c_ref, cum_ref, cumt_ref, y_ref, token, scores):
    rows = x_ref.shape[0]
    blocks = rows // BLOCK

    @pl.when(pl.program_id(0) == 0)
    def _():
        r = lax.broadcasted_iota(jnp.int32, (BLOCK, BLOCK), 0)
        c = lax.broadcasted_iota(jnp.int32, (BLOCK, BLOCK), 1)
        for k in range(blocks):
            at = slice(k * BLOCK, (k + 1) * BLOCK)
            scores[k] = jnp.where(r >= c, dot(c_ref[at, :], b_ref[at, :], NT), 0.0)

    low = low_lanes(BLOCK)
    b_t = [transposed(b_ref[k * BLOCK : (k + 1) * BLOCK, :]) for k in range(blocks)]
    for p in range(GROUP_HEADS // 2):
        ps = slice(p * LANES, (p + 1) * LANES)
        state = None
        for k in range(blocks):
            at = slice(k * BLOCK, (k + 1) * BLOCK)
            a0 = jnp.broadcast_to(cum_ref[0, at, 2 * p : 2 * p + 1], (BLOCK, LANES))
            a1 = jnp.broadcast_to(cum_ref[0, at, 2 * p + 1 : 2 * p + 2], (BLOCK, LANES))
            r0 = cumt_ref[2 * p : 2 * p + 1, at]
            r1 = cumt_ref[2 * p + 1 : 2 * p + 2, at]
            s = scores[k]
            w0 = jnp.exp2(jnp.minimum(a0 - r0, 0.0)) * s
            w1 = jnp.exp2(jnp.minimum(a1 - r1, 0.0)) * s
            x = x_ref[at, ps]
            y = dot(jnp.concatenate([w0, w1], axis=1).astype(BF16), block_diagonal(x))
            both = jnp.where(low, a0, a1)
            if k > 0:
                y = y + jnp.exp2(both) * dot(c_ref[at, :], state.astype(BF16))
            if k < blocks - 1:
                last = both[BLOCK - 1 :, :]
                fresh = dot(b_t[k], (x.astype(F32) * jnp.exp2(last - both)).astype(BF16))
                state = fresh if k == 0 else jnp.exp2(last) * state + fresh
            y_ref[at, ps] = y
    give(token)


def forward(x, b, c, cum, cumt, first, groups):
    rows = x.shape[0]
    wide = x.shape[1] // cum.shape[0]
    return pl.pallas_call(
        forward_kernel,
        grid=(groups,),
        in_specs=[
            pl.BlockSpec((rows, wide), lambda g: (0, first + g)),
            pl.BlockSpec(b.shape, lambda g: (0, 0)),
            pl.BlockSpec(c.shape, lambda g: (0, 0)),
            pl.BlockSpec((1, rows, GROUP_HEADS), lambda g: (first + g, 0, 0)),
            pl.BlockSpec((GROUP_HEADS, rows), lambda g: (first + g, 0)),
        ],
        out_specs=[pl.BlockSpec((rows, wide), lambda g: (0, g)), token_ref(True)],
        out_shape=[jax.ShapeDtypeStruct((rows, wide * groups), F32), TOKEN],
        scratch_shapes=[pltpu.VMEM((rows // BLOCK, BLOCK, BLOCK), F32)],
        compiler_params=pltpu.CompilerParams(vmem_limit_bytes=8 * MIB),
        cost_estimate=pl.CostEstimate(flops=3 * 10**9, bytes_accessed=4 * MIB, transcendentals=3 * 10**6),
        name="forward",
    )(x, b, c, cum, cumt)


def finish_kernel(y_ref, c_ref, lead_ref, own_ref, back_ref, out_ref, state_ref, token):
    state = jnp.where(pl.program_id(0) == place_in_pair(), own_ref[...].astype(F32), back_ref[...].astype(F32)).astype(BF16)
    state_ref[...] = state
    give(token)
    for p in range(GROUP_HEADS // 2):
        ps = slice(p * LANES, (p + 1) * LANES)
        lead = pair_columns(lead_ref[0], p)
        out_ref[:, ps] = (y_ref[:, ps] + lead * dot(c_ref[...], state[:, ps])).astype(BF16)


def finish(y, c, lead, own, back, first):
    rows, width = y.shape
    states, wide = own.shape
    return pl.pallas_call(
        finish_kernel,
        grid=(2,),
        in_specs=[
            pl.BlockSpec((rows, wide), lambda g: (0, g)),
            pl.BlockSpec(c.shape, lambda g: (0, 0)),
            pl.BlockSpec((1, rows, GROUP_HEADS), lambda g: (first + g, 0, 0)),
            pl.BlockSpec((states, wide), lambda g: (0, 0)),
            pl.BlockSpec((states, wide), lambda g: (0, 0)),
        ],
        out_specs=[pl.BlockSpec((rows, wide), lambda g: (0, g)), pl.BlockSpec((states, wide), lambda g: (0, g)), token_ref(True)],
        out_shape=[jax.ShapeDtypeStruct((rows, width), BF16), jax.ShapeDtypeStruct((states, width), BF16), TOKEN],
        compiler_params=pltpu.CompilerParams(vmem_limit_bytes=8 * MIB),
        cost_estimate=pl.CostEstimate(flops=3 * 10**8, bytes_accessed=4 * MIB, transcendentals=0),
        name="finish",
    )(y, c, lead, own, back)


def adjoint_kernel(dout_ref, w_ref, c_ref, lead_ref, after, gy_ref, keep_ref, send_ref, token):
    c_t = transposed(c_ref[...])
    gy = dot(dout_ref[...], w_ref[...])
    gy_ref[...] = gy.astype(BF16)
    own = []
    for p in range(GROUP_HEADS // 2):
        ps = slice(p * LANES, (p + 1) * LANES)
        scaled = gy[:, ps] * pair_columns(lead_ref[0], p)
        own.append(dot(c_t, scaled.astype(BF16)))
    own = jnp.concatenate(own, axis=1)
    mine = pl.program_id(0) == place_in_pair()
    give(token)

    @pl.when(mine)
    def _():
        keep_ref[...] = own

    @pl.when(jnp.logical_not(mine))
    def _():
        send_ref[...] = own.astype(BF16)


def adjoint(dout, w, c, lead, first, after):
    rows, model = dout.shape
    wide = w.shape[1] // lead.shape[0]
    states = c.shape[1]
    return pl.pallas_call(
        adjoint_kernel,
        grid=(2,),
        in_specs=[
            pl.BlockSpec((rows, model), lambda g: (0, 0)),
            pl.BlockSpec((model, wide), lambda g: (0, first + g)),
            pl.BlockSpec(c.shape, lambda g: (0, 0)),
            pl.BlockSpec((1, rows, GROUP_HEADS), lambda g: (first + g, 0, 0)),
            token_ref(True),
        ],
        out_specs=[
            pl.BlockSpec((rows, wide), lambda g: (0, g)),
            pl.BlockSpec((states, wide), lambda g: (0, 0)),
            pl.BlockSpec((states, wide), lambda g: (0, 0)),
            token_ref(True),
        ],
        out_shape=[
            jax.ShapeDtypeStruct((rows, 2 * wide), BF16),
            jax.ShapeDtypeStruct((states, wide), F32),
            jax.ShapeDtypeStruct((states, wide), BF16),
            TOKEN,
        ],
        compiler_params=pltpu.CompilerParams(vmem_limit_bytes=16 * MIB),
        cost_estimate=pl.CostEstimate(flops=3 * 10**9, bytes_accessed=8 * MIB, transcendentals=0),
        name="adjoint",
    )(dout, w, c, lead, after)


def turn_kernel(dout_ref, out_ref, token, *, ring):
    count = len(ring)
    tall = dout_ref.shape[1] // count
    me = lax.axis_index("ctx")
    give(token)
    for i in range(count):
        to = sum(jnp.where(me == ring[j], ring[(j + i) % count], 0) for j in range(count))
        block = dout_ref[:, pl.ds(pl.multiple_of(to * tall, LANES), tall)]
        out_ref[i * tall : (i + 1) * tall, :] = transposed(block)


def turn(dout, ring):
    rows, model = dout.shape
    return pl.pallas_call(
        functools.partial(turn_kernel, ring=ring),
        in_specs=[vmem_ref()],
        out_specs=[vmem_ref()] * 2,
        out_shape=[jax.ShapeDtypeStruct((model, rows), BF16), TOKEN],
        compiler_params=pltpu.CompilerParams(vmem_limit_bytes=12 * MIB),
        cost_estimate=pl.CostEstimate(flops=0, bytes_accessed=4 * MIB, transcendentals=0),
        name="turn",
    )(dout)


def backward_kernel(
    x_ref, gy_ref, y_ref, b_ref, c_ref, cum_ref, cumt_ref, s_ref, own_ref, back_ref, after,
    gx_ref, db_ref, dc_ref, dl_ref,
    scores, dscores, *, half,
):
    rows = x_ref.shape[0]
    blocks = rows // BLOCK
    step, steps = pl.program_id(0), pl.num_programs(0)
    r = lax.broadcasted_iota(jnp.int32, (BLOCK, BLOCK), 0)
    c = lax.broadcasted_iota(jnp.int32, (BLOCK, BLOCK), 1)
    upper = r <= c

    @pl.when(step == 0)
    def _():
        for k in range(blocks):
            at = slice(k * BLOCK, (k + 1) * BLOCK)
            scores[k] = jnp.where(upper, dot(b_ref[at, :], c_ref[at, :], NT), 0.0)
        dscores[...] = jnp.zeros_like(dscores)
        db_ref[...] = jnp.zeros_like(db_ref)
        dc_ref[...] = jnp.zeros_like(dc_ref)

    low = low_lanes(BLOCK)
    leaving = jnp.where(step + half == place_in_pair(), own_ref[...].astype(F32), back_ref[...].astype(F32))
    spots = [slice(k * BLOCK, (k + 1) * BLOCK) for k in range(blocks)]
    b_t = [transposed(b_ref[at, :]) for at in spots]
    c_t = [transposed(c_ref[at, :]) for at in spots]
    sums = [jnp.zeros((GROUP_HEADS, BLOCK), F32)] * blocks
    head_row = lax.broadcasted_iota(jnp.int32, (GROUP_HEADS, LANES), 0)
    head_half = lax.broadcasted_iota(jnp.int32, (GROUP_HEADS, LANES), 1) // (LANES // 2)
    for p in range(GROUP_HEADS // 2):
        ps = slice(p * LANES, (p + 1) * LANES)
        place = (head_row == 2 * p + head_half).astype(BF16)
        columns, tails, entering = [], [], [s_ref[:, ps].astype(F32)]
        for k, at in enumerate(spots):
            a0 = jnp.broadcast_to(cum_ref[0, at, 2 * p : 2 * p + 1], (BLOCK, LANES))
            a1 = jnp.broadcast_to(cum_ref[0, at, 2 * p + 1 : 2 * p + 2], (BLOCK, LANES))
            both = jnp.where(low, a0, a1)
            last = both[BLOCK - 1 :, :]
            columns.append((a0, a1, both, jnp.exp2(last)))
            tail = jnp.exp2(last - both)
            tails.append((tail, (x_ref[at, ps].astype(F32) * tail).astype(BF16)))
            entering.append(jnp.exp2(last) * entering[k] + dot(b_t[k], tails[k][1]))
        g = leaving[:, ps]
        for k in reversed(range(blocks)):
            at = spots[k]
            a0, a1, both, span = columns[k]
            tail, xs = tails[k]
            d0 = jnp.exp2(jnp.minimum(cumt_ref[2 * p : 2 * p + 1, at] - a0, 0.0))
            d1 = jnp.exp2(jnp.minimum(cumt_ref[2 * p + 1 : 2 * p + 2, at] - a1, 0.0))
            s = scores[k]
            x, gy = x_ref[at, ps], gy_ref[at, ps]
            g_half = g.astype(BF16)
            weights = jnp.concatenate([d0 * s, d1 * s], axis=1).astype(BF16)
            gx = dot(weights, block_diagonal(gy)) + tail * dot(b_ref[at, :], g_half)
            gx_ref[at, ps] = gx.astype(BF16)
            dw = dot(block_diagonal(x), gy, NT)
            dscores[k] += d0 * dw[:BLOCK] + d1 * dw[BLOCK:]
            db_ref[at, :] += dot(xs, g_half, NT)
            gys = (gy.astype(F32) * jnp.exp2(both)).astype(BF16)
            dc_ref[at, :] += dot(gys, entering[k].astype(BF16), NT)
            term = gy.astype(F32) * y_ref[at, ps].astype(F32) - x.astype(F32) * gx
            end = jnp.sum(entering[k + 1] * g, axis=0, keepdims=True)
            term = term + jnp.where(r == BLOCK - 1, end, 0.0)
            hi = term.astype(BF16)
            lo = (term - hi.astype(F32)).astype(BF16)
            sums[k] = sums[k] + dot(place, hi, NT) + dot(place, lo, NT)
            g = span * g + dot(c_t[k], gys)
    for k, at in enumerate(spots):
        dl_ref[:, at] = dot(sums[k], (r >= c).astype(F32), precision=EXACT)

    @pl.when(step == steps - 1)
    def _():
        for k, at in enumerate(spots):
            ds = jnp.where(upper, dscores[k], 0.0)
            db_ref[at, :] += dot(ds.astype(BF16), c_ref[at, :])
            dc_ref[at, :] += dot(ds.T.astype(BF16), b_ref[at, :])


def backward(x, gy, y, b, c, cum, cumt, entering, own, back, first, half, steps, after):
    rows = x.shape[0]
    states, wide = own.shape
    here = pl.BlockSpec((rows, wide), lambda g: (0, half + g))
    whole = pl.BlockSpec((rows, states), lambda g: (0, 0))
    return pl.pallas_call(
        functools.partial(backward_kernel, half=half),
        grid=(steps,),
        in_specs=[
            pl.BlockSpec((rows, wide), lambda g: (0, first + half + g)),
            here, here, whole, whole,
            pl.BlockSpec((1, rows, GROUP_HEADS), lambda g: (first + half + g, 0, 0)),
            pl.BlockSpec((GROUP_HEADS, rows), lambda g: (first + half + g, 0)),
            pl.BlockSpec((states, wide), lambda g: (0, half + g)),
            pl.BlockSpec((states, wide), lambda g: (0, 0)),
            pl.BlockSpec((states, wide), lambda g: (0, 0)),
            pl.BlockSpec((16, LANES), lambda g: (0, 0)),
        ],
        out_specs=[
            pl.BlockSpec((rows, wide), lambda g: (0, g)),
            whole, whole, pl.BlockSpec((GROUP_HEADS, rows), lambda g: (g, 0)),
        ],
        out_shape=[
            jax.ShapeDtypeStruct((rows, wide * steps), BF16),
            jax.ShapeDtypeStruct((rows, states), F32),
            jax.ShapeDtypeStruct((rows, states), F32),
            jax.ShapeDtypeStruct((GROUP_HEADS * steps, rows), F32),
        ],
        scratch_shapes=[pltpu.VMEM((rows // BLOCK, BLOCK, BLOCK), F32)] * 2,
        compiler_params=pltpu.CompilerParams(vmem_limit_bytes=14 * MIB),
        cost_estimate=pl.CostEstimate(flops=3 * 10**9 * steps, bytes_accessed=3 * MIB * steps, transcendentals=10**6),
        name="backward",
    )(x, gy, y, b, c, cum, cumt, entering, own, back, after)


def ring_order(count):
    if count == 8:
        return [0, 2, 4, 6, 7, 5, 3, 1]
    return list(range(count))


def on_device(x, b, c, loga, dout, w):
    count = lax.axis_size("ctx")
    rows, width = x.shape
    wide = width // 2
    eighth = 2
    ring = ring_order(count)
    tall = dout.shape[1] // count

    cum, cumt, lead, tail, keep0, tot0, send0 = start(loga.T, x, b, wide)
    keep1, tot1, send1 = ends(x, b, tail, 1, wide)
    (y0, done0), (y1, done1) = [forward(x, b, c, cum, cumt, eighth * g, eighth) for g in range(2)]
    dout_t, turned = turn(dout, ring)
    afters = [((done0,), (done1,), ()), ((), (turned,), ())]
    tots, keeps, sends, y_local = (tot0, tot1), (keep0, keep1), (send0, send1), (y0, y1)
    y_half, entering, others = [], [], []
    for g in range(2):
        own, back, other = scan(sends[g], keeps[g], tots[g], None, True, afters[g])
        y, state, finished = finish(y_local[g], c, lead, own, back, eighth * g)
        y_half.append(y)
        entering.append(state)
        others.append(other)

    flows = []
    for g in range(2):
        for f, by in enumerate((1, -1)):
            hops = [(ring[i], ring[(i + by) % count]) for i in range(count)]
            flows.append([hops, by, y_half[g][:, f * wide // 2 : (f + 1) * wide // 2], None])
    passed = []
    for step in range(count):
        for flow in flows:
            hops, by, y, got_sum = flow
            offset = (by * (count - 1 - step)) % count
            part = dot(dout_t[offset * tall : (offset + 1) * tall], y)
            if got_sum is not None:
                part = part + got_sum.astype(F32)
            flow[3] = part if step == count - 1 else lax.ppermute(part.astype(BF16), "ctx", hops)
        passed.append(flows[3][3])
    weight_grad = jnp.concatenate([flow[3] for flow in flows], axis=1)

    grads = []
    after = finished
    for g in range(2):
        gy, keep, send, after = adjoint(dout, w, c, lead, eighth * g, after)
        own, back, _ = scan(send, keep, tots[g], others[g], False, ((), (), ()))
        for h in range(2):
            late = passed[count - 5 + 2 * g + h - (0 if g == 0 else 1)]
            grads.append(
                backward(x, gy, y_half[g], b, c, cum, cumt, entering[g], own, back, eighth * g, h, 1, late)
            )
    grad_x = jnp.concatenate([g[0] for g in grads], axis=1)
    db = sum(g[1] for g in grads)
    dc = sum(g[2] for g in grads)
    dl = jnp.concatenate([g[3] for g in grads], axis=0)
    terms = jnp.concatenate([db, dc], axis=0).astype(BF16)
    summed = terms.astype(F32) + lax.ppermute(terms, "head", [(0, 1), (1, 0)]).astype(F32)
    return grad_x, summed[:rows], summed[rows:], dl.T, weight_grad


def solution(mesh):
    tokens = ("group", "ctx")
    placed = (
        P(tokens, "head"),
        P(tokens, None),
        P(tokens, None),
        P(tokens, "head"),
        P(tokens, None),
        P(None, "head"),
    )
    return jax.shard_map(
        on_device,
        mesh=mesh,
        in_specs=placed,
        out_specs=(
            P(tokens, "head"),
            P(tokens, None),
            P(tokens, None),
            P(tokens, "head"),
            P(tokens, "head"),
        ),
        check_vma=False,
    )
```

```python
import functools
import math

import jax
import jax.numpy as jnp
from jax import lax
from jax.experimental import pallas as pl
from jax.experimental.pallas import tpu as pltpu
from jax.sharding import PartitionSpec as P

BLOCK = 128
LANES = 128
GROUP_HEADS = 8
LOG2E = math.log2(math.e)
F32 = jnp.float32
BF16 = jnp.bfloat16
EXACT = lax.Precision.HIGHEST
NT = (((1,), (1,)), ((), ()))
TN = (((0,), (0,)), ((), ()))
MIB = 2**20


def dot(a, b, dims=(((1,), (0,)), ((), ())), precision=None):
    return lax.dot_general(a, b, dims, precision=precision, preferred_element_type=F32)


def low_lanes(rows):
    return lax.broadcasted_iota(jnp.int32, (rows, LANES), 1) < LANES // 2


def pair_columns(small, pair):
    rows = small.shape[0]
    even = jnp.broadcast_to(small[:, 2 * pair : 2 * pair + 1], (rows, LANES))
    odd = jnp.broadcast_to(small[:, 2 * pair + 1 : 2 * pair + 2], (rows, LANES))
    return jnp.where(low_lanes(rows), even, odd)


def transposed(x):
    return x.astype(F32).T.astype(BF16)


def place_in_pair():
    return lax.rem(lax.axis_index("ctx"), 2)


def pairs_before(up):
    me, count = lax.axis_index("ctx"), lax.axis_size("ctx")
    return me // 2 if up else (count - 1 - me) // 2


def vmem_ref():
    return pl.BlockSpec(memory_space=pltpu.VMEM)


TOKEN = jax.ShapeDtypeStruct((8, LANES), F32)


def token_ref(like=TOKEN):
    return pl.BlockSpec((8 if like.dtype == F32 else 16, LANES), lambda *g: (0, 0))


def give(token):
    token[...] = jnp.zeros_like(token)


def log_rows(t):
    hi = t.astype(BF16).astype(F32)
    mid = (t - hi).astype(BF16).astype(F32)
    lo = t - hi - mid
    row = lax.broadcasted_iota(jnp.int32, t.shape, 0)
    pieces = jnp.where(row == 0, hi, jnp.where(row == 1, mid, jnp.where(row == 2, lo, 0.0)))
    return jnp.concatenate([pieces, jnp.zeros_like(pieces)], axis=0).astype(BF16)


def end_states(x_ref, b_t, tail, total, keep_ref, tot_ref, send_ref, own):
    rows, width = x_ref.shape
    states = b_t.shape[0]
    half = width // 2
    heads = width // (LANES // 2)
    for p in range(heads // 2):
        ps = slice(p * LANES, (p + 1) * LANES)
        xs = (x_ref[:, ps].astype(F32) * pair_columns(tail, p)).astype(BF16)
        own[0:states, ps] = dot(b_t, xs)
        own[states : states + 8, ps] = pair_columns(total, p)
    q = place_in_pair()
    mine = pl.ds(pl.multiple_of(q * half, LANES), half)
    other = pl.ds(pl.multiple_of((1 - q) * half, LANES), half)
    keep_ref[...] = own[0:states, mine]
    tot_ref[...] = own[states : states + 8, mine]
    send_ref[0:states, :] = own[0:states, other].astype(BF16)
    send_ref[states : states + 16, :] = log_rows(own[states : states + 8, other])


def start_kernel(
    loga_ref, x_ref, b_ref, cum_ref, cumt_ref, lead_ref, keep_ref, tot_ref, send_ref, own
):
    heads, rows = loga_ref.shape
    r = lax.broadcasted_iota(jnp.int32, (BLOCK, BLOCK), 0)
    c = lax.broadcasted_iota(jnp.int32, (BLOCK, BLOCK), 1)
    base = jnp.zeros((1, heads), F32)
    whole = []
    for k in range(rows // BLOCK):
        at = slice(k * BLOCK, (k + 1) * BLOCK)
        logs = loga_ref[:, at] * LOG2E
        cum = dot((r >= c).astype(F32), logs, NT, precision=EXACT)
        for g in range(heads // GROUP_HEADS):
            cum_ref[g, at, :] = cum[:, g * GROUP_HEADS : (g + 1) * GROUP_HEADS]
        cumt_ref[:, at] = dot(logs, (r <= c).astype(F32), precision=EXACT)
        whole.append(cum + base)
        base = base + cum[BLOCK - 1 :, :]
    whole = jnp.concatenate(whole, axis=0)
    lead, tail = jnp.exp2(whole), jnp.exp2(base - whole)
    for g in range(heads // GROUP_HEADS):
        hs = slice(g * GROUP_HEADS, (g + 1) * GROUP_HEADS)
        lead_ref[g] = lead[:, hs]
    total = jnp.broadcast_to(base, (8, heads))
    end_states(x_ref, transposed(b_ref[...]), tail, total, keep_ref, tot_ref, send_ref, own)


def start(logs, x, b):
    heads, rows = logs.shape
    width = x.shape[1]
    states = b.shape[1]
    groups = heads // GROUP_HEADS
    return pl.pallas_call(
        start_kernel,
        grid=(1,),
        in_specs=[
            pl.BlockSpec((heads, rows), lambda i: (0, 0)),
            pl.BlockSpec((rows, width), lambda i: (0, 0)),
            pl.BlockSpec(b.shape, lambda i: (0, 0)),
        ],
        out_specs=[vmem_ref()] * 6,
        out_shape=[
            jax.ShapeDtypeStruct((groups, rows, GROUP_HEADS), F32),
            jax.ShapeDtypeStruct((heads, rows), F32),
            jax.ShapeDtypeStruct((groups, rows, GROUP_HEADS), F32),
            jax.ShapeDtypeStruct((states, width // 2), F32),
            jax.ShapeDtypeStruct((8, width // 2), F32),
            jax.ShapeDtypeStruct((states + 16, width // 2), BF16),
        ],
        scratch_shapes=[pltpu.VMEM((states + 8, width), F32)],
        compiler_params=pltpu.CompilerParams(vmem_limit_bytes=20 * MIB),
        cost_estimate=pl.CostEstimate(flops=10**9, bytes_accessed=4 * MIB, transcendentals=10**5),
        name="start",
    )(logs, x, b)


def joined_kernel(keep_ref, got_ref, tot_ref, other_ref, *refs, first_is, from_message):
    out_ref, both_ref, other_out, token = refs[-4:]
    give(token)
    states = keep_ref.shape[0]
    got = got_ref[0:states, :].astype(F32)
    if from_message:
        pieces = got_ref[states : states + 16, :].astype(F32)
        other = pieces[0:1] + pieces[1:2] + pieces[2:3]
    else:
        other = other_ref[0:1, :]
    mine = tot_ref[0:1, :]
    first = place_in_pair() == first_is
    later = jnp.exp2(jnp.where(first, other, mine))
    keep = keep_ref[...]
    both = jnp.where(first, later * keep + got, later * got + keep)
    both_ref[...] = both
    out_ref[0:states, :] = both.astype(BF16)
    out_ref[states : states + 16, :] = log_rows(jnp.broadcast_to(mine + other, (8, keep.shape[1])))
    other_out[...] = jnp.broadcast_to(other, other_out.shape)


def small_kernel(body, name, shapes, arrays, after):
    return pl.pallas_call(
        body,
        grid=(1,),
        in_specs=[pl.BlockSpec(a.shape, lambda i: (0, 0)) for a in arrays] + [token_ref(a) for a in after],
        out_specs=[pl.BlockSpec(shape, lambda i: (0, 0)) for shape, _ in shapes] + [token_ref()],
        out_shape=[jax.ShapeDtypeStruct(*s) for s in shapes] + [TOKEN],
        compiler_params=pltpu.CompilerParams(vmem_limit_bytes=4 * MIB),
        cost_estimate=pl.CostEstimate(flops=10**6, bytes_accessed=MIB, transcendentals=0),
        name=name,
    )(*arrays, *after)


def joined(keep, got, tot, other, up, after):
    states, half = keep.shape
    body = functools.partial(joined_kernel, first_is=0 if up else 1, from_message=other is None)
    shapes = [((states + 16, half), BF16), ((states, half), F32), ((8, half), F32)]
    return small_kernel(body, "joined", shapes, (keep, got, tot, tot if other is None else other), after)


def carry_kernel(both_ref, in_ref, tot_ref, other_ref, *refs, up):
    out_ref, token = refs[-2:]
    give(token)
    states = both_ref.shape[0]
    seen = (pairs_before(up) > 0).astype(F32)
    span = jnp.exp2(tot_ref[0:1, :] + other_ref[0:1, :]) * seen
    out_ref[...] = (both_ref[...] + span * in_ref[0:states, :].astype(F32)).astype(BF16)


def carry(both, into, tot, other, up, after):
    body = functools.partial(carry_kernel, up=up)
    return small_kernel(body, "carry", [(both.shape, BF16)], (both, into, tot, other), after)


def entered_kernel(keep_ref, got_ref, tot_ref, other_ref, near_ref, *refs, up, far):
    own_ref, partner_ref, token = refs[-3:]
    give(token)
    states = keep_ref.shape[0]
    enter = near_ref[0:states, :].astype(F32)
    if far:
        pieces = near_ref[states : states + 16, :].astype(F32)
        span = jnp.exp2(pieces[0:1] + pieces[1:2] + pieces[2:3])
        enter = enter + jnp.where(pairs_before(up) > 1, span * refs[0][...].astype(F32), 0.0)
    enter = jnp.where(pairs_before(up) > 0, enter, 0.0)
    mine, other = jnp.exp2(tot_ref[0:1, :]), jnp.exp2(other_ref[0:1, :])
    first = place_in_pair() == (0 if up else 1)
    after_me = mine * enter + keep_ref[...]
    after_other = other * enter + got_ref[0:states, :].astype(F32)
    own_ref[...] = jnp.where(first, enter, after_other).astype(BF16)
    partner_ref[...] = jnp.where(first, after_me, enter).astype(BF16)


def entered(keep, got, tot, other, near, far, up, after):
    body = functools.partial(entered_kernel, up=up, far=far is not None)
    shapes = [(keep.shape, BF16)] * 2
    arrays = (keep, got, tot, other, near) + (() if far is None else (far,))
    return small_kernel(body, "entered", shapes, arrays, after)


def hop(x, up, by, wrap):
    count = lax.axis_size("ctx")
    by = 2 * by if up else -2 * by
    return lax.ppermute(x, "ctx", [(i, (i + by) % count) for i in range(count) if wrap or 0 <= i + by < count])


def swap(x):
    return lax.ppermute(x, "ctx", [(i, i ^ 1) for i in range(lax.axis_size("ctx"))])


def reach(message, both, tot, other, up, after, wrap):
    count = lax.axis_size("ctx")
    near = hop(message, up, 1, wrap[0])
    if count == 8:
        out, token = carry(both, near, tot, other, up, after)
        return near, hop(out, up, 2, wrap[1]), token
    for _ in range(count // 2 - 2):
        out, token = carry(both, near, tot, other, up, after)
        near = hop(out, up, 1, wrap[0])
    return near, None, token


def block_diagonal(pair):
    low = low_lanes(pair.shape[0])
    wide = pair.astype(F32)
    zero = jnp.zeros_like(wide)
    return jnp.concatenate([jnp.where(low, wide, zero), jnp.where(low, zero, wide)], axis=0).astype(BF16)


def forward_kernel(x_ref, b_ref, c_ref, cum_ref, cumt_ref, after, y_ref, token, scores):
    rows = x_ref.shape[0]
    blocks = rows // BLOCK

    @pl.when(pl.program_id(0) == 0)
    def _():
        r = lax.broadcasted_iota(jnp.int32, (BLOCK, BLOCK), 0)
        c = lax.broadcasted_iota(jnp.int32, (BLOCK, BLOCK), 1)
        for k in range(blocks):
            at = slice(k * BLOCK, (k + 1) * BLOCK)
            scores[k] = jnp.where(r >= c, dot(c_ref[at, :], b_ref[at, :], NT), 0.0)

    low = low_lanes(BLOCK)
    b_t = [transposed(b_ref[k * BLOCK : (k + 1) * BLOCK, :]) for k in range(blocks)]
    for p in range(GROUP_HEADS // 2):
        ps = slice(p * LANES, (p + 1) * LANES)
        state = None
        for k in range(blocks):
            at = slice(k * BLOCK, (k + 1) * BLOCK)
            a0 = jnp.broadcast_to(cum_ref[0, at, 2 * p : 2 * p + 1], (BLOCK, LANES))
            a1 = jnp.broadcast_to(cum_ref[0, at, 2 * p + 1 : 2 * p + 2], (BLOCK, LANES))
            r0 = cumt_ref[2 * p : 2 * p + 1, at]
            r1 = cumt_ref[2 * p + 1 : 2 * p + 2, at]
            s = scores[k]
            w0 = jnp.exp2(jnp.minimum(a0 - r0, 0.0)) * s
            w1 = jnp.exp2(jnp.minimum(a1 - r1, 0.0)) * s
            x = x_ref[at, ps]
            y = dot(jnp.concatenate([w0, w1], axis=1).astype(BF16), block_diagonal(x))
            both = jnp.where(low, a0, a1)
            if k > 0:
                y = y + jnp.exp2(both) * dot(c_ref[at, :], state.astype(BF16))
            if k < blocks - 1:
                last = both[BLOCK - 1 :, :]
                fresh = dot(b_t[k], (x.astype(F32) * jnp.exp2(last - both)).astype(BF16))
                state = fresh if k == 0 else jnp.exp2(last) * state + fresh
            y_ref[at, ps] = y
    give(token)


def forward(x, b, c, cum, cumt, first, groups, after):
    rows = x.shape[0]
    wide = x.shape[1] // cum.shape[0]
    return pl.pallas_call(
        forward_kernel,
        grid=(groups,),
        in_specs=[
            pl.BlockSpec((rows, wide), lambda g: (0, first + g)),
            pl.BlockSpec(b.shape, lambda g: (0, 0)),
            pl.BlockSpec(c.shape, lambda g: (0, 0)),
            pl.BlockSpec((1, rows, GROUP_HEADS), lambda g: (first + g, 0, 0)),
            pl.BlockSpec((GROUP_HEADS, rows), lambda g: (first + g, 0)),
            token_ref(),
        ],
        out_specs=[pl.BlockSpec((rows, wide), lambda g: (0, g)), token_ref()],
        out_shape=[jax.ShapeDtypeStruct((rows, wide * groups), F32), TOKEN],
        scratch_shapes=[pltpu.VMEM((rows // BLOCK, BLOCK, BLOCK), F32)],
        compiler_params=pltpu.CompilerParams(vmem_limit_bytes=8 * MIB),
        cost_estimate=pl.CostEstimate(flops=3 * 10**9, bytes_accessed=4 * MIB, transcendentals=3 * 10**6),
        name="forward",
    )(x, b, c, cum, cumt, after)


def finish_kernel(y_ref, c_ref, lead_ref, own_ref, back_ref, after, out_ref, state_ref, token, *, half):
    state = jnp.where(half == place_in_pair(), own_ref[...].astype(F32), back_ref[...].astype(F32)).astype(BF16)
    state_ref[...] = state
    give(token)
    for p in range(GROUP_HEADS // 2):
        ps = slice(p * LANES, (p + 1) * LANES)
        lead = pair_columns(lead_ref[0], p)
        out_ref[:, ps] = (y_ref[:, ps] + lead * dot(c_ref[...], state[:, ps])).astype(BF16)


def finish(y, c, lead, own, back, half, after):
    rows, width = y.shape
    states = own.shape[0]
    wide = width // 2
    first = 2 * half
    return pl.pallas_call(
        functools.partial(finish_kernel, half=half),
        grid=(2,),
        in_specs=[
            pl.BlockSpec((rows, wide), lambda g: (0, g)),
            pl.BlockSpec(c.shape, lambda g: (0, 0)),
            pl.BlockSpec((1, rows, GROUP_HEADS), lambda g: (first + g, 0, 0)),
            pl.BlockSpec((states, wide), lambda g: (0, g)),
            pl.BlockSpec((states, wide), lambda g: (0, g)),
            token_ref(),
        ],
        out_specs=[pl.BlockSpec((rows, wide), lambda g: (0, g)), pl.BlockSpec((states, wide), lambda g: (0, g)), token_ref()],
        out_shape=[jax.ShapeDtypeStruct((rows, width), BF16), jax.ShapeDtypeStruct((states, width), BF16), TOKEN],
        compiler_params=pltpu.CompilerParams(vmem_limit_bytes=8 * MIB),
        cost_estimate=pl.CostEstimate(flops=3 * 10**8, bytes_accessed=4 * MIB, transcendentals=0),
        name="finish",
    )(y, c, lead, own, back, after)


def adjoint_kernel(dout_ref, w_ref, c_ref, lead_ref, after, *refs, group):
    gy_ref, keep_ref, send_ref, token = refs[-4:]
    c_t = transposed(c_ref[...])
    gy = dot(dout_ref[...], w_ref[...])
    gy_ref[...] = gy.astype(BF16)
    give(token)
    mine = group == place_in_pair()
    for p in range(GROUP_HEADS // 2):
        ps = slice(p * LANES, (p + 1) * LANES)
        scaled = gy[:, ps] * pair_columns(lead_ref[0], p)
        own = dot(c_t, scaled.astype(BF16))
        if group == 0:
            keep_ref[:, ps] = own
            send_ref[:, ps] = own.astype(BF16)
        else:
            keep_ref[:, ps] = jnp.where(mine, own, refs[0][:, ps])
            send_ref[:, ps] = jnp.where(mine, refs[1][:, ps].astype(F32), own).astype(BF16)


def adjoint(dout, w, c, lead, group, after, before):
    rows, model = dout.shape
    wide = w.shape[1] // lead.shape[0]
    first = 2 * group
    states = c.shape[1]
    state = pl.BlockSpec((states, wide), lambda g: (0, g))
    return pl.pallas_call(
        functools.partial(adjoint_kernel, group=group),
        grid=(2,),
        in_specs=[
            pl.BlockSpec((rows, model), lambda g: (0, 0)),
            pl.BlockSpec((model, wide), lambda g: (0, first + g)),
            pl.BlockSpec(c.shape, lambda g: (0, 0)),
            pl.BlockSpec((1, rows, GROUP_HEADS), lambda g: (first + g, 0, 0)),
            token_ref(),
        ] + [state] * len(before),
        out_specs=[pl.BlockSpec((rows, wide), lambda g: (0, g)), state, state, token_ref()],
        out_shape=[
            jax.ShapeDtypeStruct((rows, 2 * wide), BF16),
            jax.ShapeDtypeStruct((states, 2 * wide), F32),
            jax.ShapeDtypeStruct((states, 2 * wide), BF16),
            TOKEN,
        ],
        compiler_params=pltpu.CompilerParams(vmem_limit_bytes=16 * MIB),
        cost_estimate=pl.CostEstimate(flops=3 * 10**9, bytes_accessed=8 * MIB, transcendentals=0),
        name="adjoint",
    )(dout, w, c, lead, after, *before)


def turn_kernel(dout_ref, after, out_ref, token, *, ring):
    count = len(ring)
    tall = dout_ref.shape[1] // count
    me = lax.axis_index("ctx")
    give(token)
    for i in range(count):
        to = sum(jnp.where(me == ring[j], ring[(j + i) % count], 0) for j in range(count))
        block = dout_ref[:, pl.ds(pl.multiple_of(to * tall, LANES), tall)]
        out_ref[i * tall : (i + 1) * tall, :] = transposed(block)


def turn(dout, ring, after):
    rows, model = dout.shape
    return pl.pallas_call(
        functools.partial(turn_kernel, ring=ring),
        grid=(1,),
        in_specs=[pl.BlockSpec(dout.shape, lambda i: (0, 0)), token_ref()],
        out_specs=[pl.BlockSpec((model, rows), lambda i: (0, 0)), token_ref()],
        out_shape=[jax.ShapeDtypeStruct((model, rows), BF16), TOKEN],
        compiler_params=pltpu.CompilerParams(vmem_limit_bytes=12 * MIB),
        cost_estimate=pl.CostEstimate(flops=0, bytes_accessed=4 * MIB, transcendentals=0),
        name="turn",
    )(dout, after)


def backward_kernel(
    x_ref, gy_ref, y_ref, b_ref, c_ref, cum_ref, cumt_ref, s_ref, own_ref, back_ref, after,
    *refs, group, more,
):
    gx_ref, db_ref, dc_ref, dl_ref, scores, dscores = refs[-6:]
    rows = x_ref.shape[0]
    blocks = rows // BLOCK
    step, steps = pl.program_id(0), pl.num_programs(0)
    r = lax.broadcasted_iota(jnp.int32, (BLOCK, BLOCK), 0)
    c = lax.broadcasted_iota(jnp.int32, (BLOCK, BLOCK), 1)
    upper = r <= c

    @pl.when(step == 0)
    def _():
        for k in range(blocks):
            at = slice(k * BLOCK, (k + 1) * BLOCK)
            scores[k] = jnp.where(upper, dot(b_ref[at, :], c_ref[at, :], NT), 0.0)
        dscores[...] = jnp.zeros_like(dscores)
        db_ref[...] = refs[1][...] if more else jnp.zeros_like(db_ref)
        dc_ref[...] = refs[2][...] if more else jnp.zeros_like(dc_ref)

    low = low_lanes(BLOCK)
    leaving = jnp.where(group == place_in_pair(), own_ref[...].astype(F32), back_ref[...].astype(F32))
    spots = [slice(k * BLOCK, (k + 1) * BLOCK) for k in range(blocks)]
    b_t = [transposed(b_ref[at, :]) for at in spots]
    c_t = [transposed(c_ref[at, :]) for at in spots]
    sums = [jnp.zeros((GROUP_HEADS, BLOCK), F32)] * blocks
    head_row = lax.broadcasted_iota(jnp.int32, (GROUP_HEADS, LANES), 0)
    head_half = lax.broadcasted_iota(jnp.int32, (GROUP_HEADS, LANES), 1) // (LANES // 2)
    for p in range(GROUP_HEADS // 2):
        ps = slice(p * LANES, (p + 1) * LANES)
        place = (head_row == 2 * p + head_half).astype(BF16)
        columns, tails, entering = [], [], [s_ref[:, ps].astype(F32)]
        for k, at in enumerate(spots):
            a0 = jnp.broadcast_to(cum_ref[0, at, 2 * p : 2 * p + 1], (BLOCK, LANES))
            a1 = jnp.broadcast_to(cum_ref[0, at, 2 * p + 1 : 2 * p + 2], (BLOCK, LANES))
            both = jnp.where(low, a0, a1)
            last = both[BLOCK - 1 :, :]
            columns.append((a0, a1, both, jnp.exp2(last)))
            tail = jnp.exp2(last - both)
            tails.append((tail, (x_ref[at, ps].astype(F32) * tail).astype(BF16)))
            entering.append(jnp.exp2(last) * entering[k] + dot(b_t[k], tails[k][1]))
        g = leaving[:, ps]
        for k in reversed(range(blocks)):
            at = spots[k]
            a0, a1, both, span = columns[k]
            tail, xs = tails[k]
            d0 = jnp.exp2(jnp.minimum(cumt_ref[2 * p : 2 * p + 1, at] - a0, 0.0))
            d1 = jnp.exp2(jnp.minimum(cumt_ref[2 * p + 1 : 2 * p + 2, at] - a1, 0.0))
            s = scores[k]
            x, gy = x_ref[at, ps], gy_ref[at, ps]
            g_half = g.astype(BF16)
            weights = jnp.concatenate([d0 * s, d1 * s], axis=1).astype(BF16)
            gx = dot(weights, block_diagonal(gy)) + tail * dot(b_ref[at, :], g_half)
            gx_ref[at, ps] = gx.astype(BF16)
            dw = dot(block_diagonal(x), gy, NT)
            dscores[k] += d0 * dw[:BLOCK] + d1 * dw[BLOCK:]
            db_ref[at, :] += dot(xs, g_half, NT)
            gys = (gy.astype(F32) * jnp.exp2(both)).astype(BF16)
            dc_ref[at, :] += dot(gys, entering[k].astype(BF16), NT)
            term = gy.astype(F32) * y_ref[at, ps].astype(F32) - x.astype(F32) * gx
            end = jnp.sum(entering[k + 1] * g, axis=0, keepdims=True)
            term = term + jnp.where(r == BLOCK - 1, end, 0.0)
            hi = term.astype(BF16)
            lo = (term - hi.astype(F32)).astype(BF16)
            sums[k] = sums[k] + dot(place, hi, NT) + dot(place, lo, NT)
            g = span * g + dot(c_t[k], gys)
    for k, at in enumerate(spots):
        dl_ref[:, at] = dot(sums[k], (r >= c).astype(F32), precision=EXACT)

    @pl.when(step == steps - 1)
    def _():
        for k, at in enumerate(spots):
            ds = jnp.where(upper, dscores[k], 0.0)
            db_ref[at, :] += dot(ds.astype(BF16), c_ref[at, :])
            dc_ref[at, :] += dot(ds.T.astype(BF16), b_ref[at, :])


def backward(x, gy, y, b, c, cum, cumt, entering, own, back, group, half, after, grads):
    rows, width = x.shape
    states = own.shape[0]
    wide = own.shape[1] // 2
    spot = 2 * group + half
    heads = GROUP_HEADS * cum.shape[0]
    here = pl.BlockSpec((rows, wide), lambda g: (0, half))
    whole = pl.BlockSpec((rows, states), lambda g: (0, 0))
    left = pl.BlockSpec(memory_space=pl.ANY)
    return pl.pallas_call(
        functools.partial(backward_kernel, group=group, more=bool(grads)),
        grid=(1,),
        in_specs=[
            pl.BlockSpec((rows, wide), lambda g: (0, spot)),
            here, here, whole, whole,
            pl.BlockSpec((1, rows, GROUP_HEADS), lambda g: (spot, 0, 0)),
            pl.BlockSpec((GROUP_HEADS, rows), lambda g: (spot, 0)),
            pl.BlockSpec((states, wide), lambda g: (0, half)),
            pl.BlockSpec((states, wide), lambda g: (0, half)),
            pl.BlockSpec((states, wide), lambda g: (0, half)),
            token_ref(after),
        ] + ([left, whole, whole, left] if grads else []),
        out_specs=[
            pl.BlockSpec((rows, wide), lambda g: (0, spot)),
            whole, whole, pl.BlockSpec((GROUP_HEADS, rows), lambda g: (spot, 0)),
        ],
        out_shape=[
            jax.ShapeDtypeStruct((rows, width), BF16),
            jax.ShapeDtypeStruct((rows, states), F32),
            jax.ShapeDtypeStruct((rows, states), F32),
            jax.ShapeDtypeStruct((heads, rows), F32),
        ],
        scratch_shapes=[pltpu.VMEM((rows // BLOCK, BLOCK, BLOCK), F32)] * 2,
        input_output_aliases={11: 0, 14: 3} if grads else {},
        compiler_params=pltpu.CompilerParams(vmem_limit_bytes=14 * MIB),
        cost_estimate=pl.CostEstimate(flops=3 * 10**9, bytes_accessed=3 * MIB, transcendentals=10**6),
        name="backward",
    )(x, gy, y, b, c, cum, cumt, entering, own, back, after, *grads)


def close_kernel(dout_ref, y_ref, got_ref, *refs):
    refs[-1][...] = dot(dout_ref[...], y_ref[...]) + got_ref[...].astype(F32)


def close(dout_t, y, got, flow, flows, before):
    tall, wide = got.shape
    rows = dout_t.shape[1]
    return pl.pallas_call(
        close_kernel,
        grid=(1,),
        in_specs=[
            pl.BlockSpec((tall, rows), lambda i: (0, 0)),
            pl.BlockSpec((rows, wide), lambda i: (0, flow % 2)),
            pl.BlockSpec((tall, wide), lambda i: (0, 0)),
        ] + [pl.BlockSpec(memory_space=pl.ANY)] * len(before),
        out_specs=pl.BlockSpec((tall, wide), lambda i: (0, flow)),
        out_shape=jax.ShapeDtypeStruct((tall, wide * flows), F32),
        input_output_aliases={3: 0} if before else {},
        compiler_params=pltpu.CompilerParams(vmem_limit_bytes=6 * MIB),
        cost_estimate=pl.CostEstimate(flops=2 * 10**8, bytes_accessed=MIB, transcendentals=0),
        name="close",
    )(dout_t, y, got, *before)


def ring_order(count):
    if count == 8:
        return [0, 2, 4, 6, 7, 5, 3, 1]
    return list(range(count))


def on_device(x, b, c, loga, dout, w):
    count = lax.axis_size("ctx")
    rows, width = x.shape
    wide = width // 2
    eighth = 2
    ring = ring_order(count)
    tall = dout.shape[1] // count

    cum, cumt, lead, keep, tot, send = start(loga.T, x, b)
    got = swap(send)
    gy0, *ends, token = adjoint(dout, w, c, lead, 0, tot, ())
    message, both, other, token = joined(keep, got, tot, None, True, (token,))
    gy1, keep_b, send_b, token = adjoint(dout, w, c, lead, 1, token, ends)
    gys = (gy0, gy1)
    near, far, token = reach(message, both, tot, other, True, (token,), (True, False))
    got_b = swap(send_b)
    y0, token = forward(x, b, c, cum, cumt, 0, eighth, token)
    message_b, both_b, _, token = joined(keep_b, got_b, tot, other, False, (token,))
    y1, token = forward(x, b, c, cum, cumt, eighth, eighth, token)
    dout_t, token = turn(dout, ring, token)
    own, partners, token = entered(keep, got, tot, other, near, far, True, (token,))
    back = swap(partners)
    near_b, far_b, token = reach(message_b, both_b, tot, other, False, (token,), (False, True))
    y_half, entering = [], []
    for g, y in enumerate((y0, y1)):
        y, state, token = finish(y, c, lead, own, back, g, token)
        y_half.append(y)
        entering.append(state)

    flows = []
    for g in range(2):
        for f, by in enumerate((1, -1)):
            hops = [(ring[i], ring[(i + by) % count]) for i in range(count)]
            flows.append([hops, by, y_half[g][:, f * wide // 2 : (f + 1) * wide // 2], None])
    passed = []
    for step in range(count - 1):
        for flow in flows:
            hops, by, y, got_sum = flow
            offset = (by * (count - 1 - step)) % count
            part = dot(dout_t[offset * tall : (offset + 1) * tall], y)
            if got_sum is not None:
                part = part + got_sum.astype(F32)
            flow[3] = lax.ppermute(part.astype(BF16), "ctx", hops)
        passed.append([flow[3] for flow in flows])
    before = ()
    for f, flow in enumerate(flows):
        before = (close(dout_t, y_half[f // 2], flow[3], f, len(flows), before),)
    weight_grad = before[0]

    own_b, partners_b, _ = entered(keep_b, got_b, tot, other, near_b, far_b, False, (passed[0][1],))
    back_b = swap(partners_b)
    grads = ()
    late = ((1, 3), (2, 3), (3, 3), (4, 3))
    for g in range(2):
        for h in range(2):
            step, f = late[2 * g + h]
            grads = backward(x, gys[g], y_half[g], b, c, cum, cumt, entering[g], own_b, back_b, g, h, passed[step][f], grads)
    grad_x, db, dc, dl = grads
    terms = jnp.concatenate([db, dc], axis=0).astype(BF16)
    summed = terms.astype(F32) + lax.ppermute(terms, "head", [(0, 1), (1, 0)]).astype(F32)
    return grad_x, summed[:rows], summed[rows:], dl.T, weight_grad


def solution(mesh):
    tokens = ("group", "ctx")
    placed = (
        P(tokens, "head"),
        P(tokens, None),
        P(tokens, None),
        P(tokens, "head"),
        P(tokens, None),
        P(None, "head"),
    )
    return jax.shard_map(
        on_device,
        mesh=mesh,
        in_specs=placed,
        out_specs=(
            P(tokens, "head"),
            P(tokens, None),
            P(tokens, None),
            P(tokens, "head"),
            P(tokens, "head"),
        ),
        check_vma=False,
    )
```

```python
import functools
import math

import jax
import jax.numpy as jnp
from jax import lax
from jax.experimental import pallas as pl
from jax.experimental.pallas import tpu as pltpu
from jax.sharding import PartitionSpec as P

BLOCK = 128
LANES = 128
GROUP_HEADS = 8
LOG2E = math.log2(math.e)
F32 = jnp.float32
BF16 = jnp.bfloat16
EXACT = lax.Precision.HIGHEST
NT = (((1,), (1,)), ((), ()))
TN = (((0,), (0,)), ((), ()))
MIB = 2**20


def dot(a, b, dims=(((1,), (0,)), ((), ())), precision=None):
    return lax.dot_general(a, b, dims, precision=precision, preferred_element_type=F32)


def low_lanes(rows):
    return lax.broadcasted_iota(jnp.int32, (rows, LANES), 1) < LANES // 2


def pair_columns(small, pair):
    rows = small.shape[0]
    even = jnp.broadcast_to(small[:, 2 * pair : 2 * pair + 1], (rows, LANES))
    odd = jnp.broadcast_to(small[:, 2 * pair + 1 : 2 * pair + 2], (rows, LANES))
    return jnp.where(low_lanes(rows), even, odd)


def transposed(x):
    return x.astype(F32).T.astype(BF16)


def place_in_pair():
    return lax.rem(lax.axis_index("ctx"), 2)


def pairs_before(up):
    me, count = lax.axis_index("ctx"), lax.axis_size("ctx")
    return me // 2 if up else (count - 1 - me) // 2


def vmem_ref():
    return pl.BlockSpec(memory_space=pltpu.VMEM)


TOKEN = jax.ShapeDtypeStruct((8, LANES), F32)


def token_ref(like=TOKEN):
    return pl.BlockSpec((8 if like.dtype == F32 else 16, LANES), lambda *g: (0, 0))


def give(token):
    token[...] = jnp.zeros_like(token)


def log_rows(t):
    hi = t.astype(BF16).astype(F32)
    mid = (t - hi).astype(BF16).astype(F32)
    lo = t - hi - mid
    row = lax.broadcasted_iota(jnp.int32, t.shape, 0)
    pieces = jnp.where(row == 0, hi, jnp.where(row == 1, mid, jnp.where(row == 2, lo, 0.0)))
    return jnp.concatenate([pieces, jnp.zeros_like(pieces)], axis=0).astype(BF16)


def end_states(x_ref, b_t, tail, total, keep_ref, tot_ref, send_ref, own):
    rows, width = x_ref.shape
    states = b_t.shape[0]
    half = width // 2
    heads = width // (LANES // 2)
    for p in range(heads // 2):
        ps = slice(p * LANES, (p + 1) * LANES)
        xs = (x_ref[:, ps].astype(F32) * pair_columns(tail, p)).astype(BF16)
        own[0:states, ps] = dot(b_t, xs)
        own[states : states + 8, ps] = pair_columns(total, p)
    q = place_in_pair()
    mine = pl.ds(pl.multiple_of(q * half, LANES), half)
    other = pl.ds(pl.multiple_of((1 - q) * half, LANES), half)
    keep_ref[...] = own[0:states, mine]
    tot_ref[...] = own[states : states + 8, mine]
    send_ref[0:states, :] = own[0:states, other].astype(BF16)
    send_ref[states : states + 16, :] = log_rows(own[states : states + 8, other])


def start_kernel(
    loga_ref, x_ref, b_ref, cum_ref, cumt_ref, lead_ref, keep_ref, tot_ref, send_ref, own
):
    heads, rows = loga_ref.shape
    r = lax.broadcasted_iota(jnp.int32, (BLOCK, BLOCK), 0)
    c = lax.broadcasted_iota(jnp.int32, (BLOCK, BLOCK), 1)
    base = jnp.zeros((1, heads), F32)
    whole = []
    for k in range(rows // BLOCK):
        at = slice(k * BLOCK, (k + 1) * BLOCK)
        logs = loga_ref[:, at] * LOG2E
        cum = dot((r >= c).astype(F32), logs, NT, precision=EXACT)
        for g in range(heads // GROUP_HEADS):
            cum_ref[g, at, :] = cum[:, g * GROUP_HEADS : (g + 1) * GROUP_HEADS]
        cumt_ref[:, at] = dot(logs, (r <= c).astype(F32), precision=EXACT)
        whole.append(cum + base)
        base = base + cum[BLOCK - 1 :, :]
    whole = jnp.concatenate(whole, axis=0)
    lead, tail = jnp.exp2(whole), jnp.exp2(base - whole)
    for g in range(heads // GROUP_HEADS):
        hs = slice(g * GROUP_HEADS, (g + 1) * GROUP_HEADS)
        lead_ref[g] = lead[:, hs]
    total = jnp.broadcast_to(base, (8, heads))
    end_states(x_ref, transposed(b_ref[...]), tail, total, keep_ref, tot_ref, send_ref, own)


def start(logs, x, b):
    heads, rows = logs.shape
    width = x.shape[1]
    states = b.shape[1]
    groups = heads // GROUP_HEADS
    return pl.pallas_call(
        start_kernel,
        grid=(1,),
        in_specs=[
            pl.BlockSpec((heads, rows), lambda i: (0, 0)),
            pl.BlockSpec((rows, width), lambda i: (0, 0)),
            pl.BlockSpec(b.shape, lambda i: (0, 0)),
        ],
        out_specs=[vmem_ref()] * 6,
        out_shape=[
            jax.ShapeDtypeStruct((groups, rows, GROUP_HEADS), F32),
            jax.ShapeDtypeStruct((heads, rows), F32),
            jax.ShapeDtypeStruct((groups, rows, GROUP_HEADS), F32),
            jax.ShapeDtypeStruct((states, width // 2), F32),
            jax.ShapeDtypeStruct((8, width // 2), F32),
            jax.ShapeDtypeStruct((states + 16, width // 2), BF16),
        ],
        scratch_shapes=[pltpu.VMEM((states + 8, width), F32)],
        compiler_params=pltpu.CompilerParams(vmem_limit_bytes=20 * MIB),
        cost_estimate=pl.CostEstimate(flops=10**9, bytes_accessed=4 * MIB, transcendentals=10**5),
        name="start",
    )(logs, x, b)


def joined_kernel(keep_ref, got_ref, tot_ref, other_ref, *refs, first_is, from_message):
    out_ref, both_ref, other_out, token = refs[-4:]
    give(token)
    states = keep_ref.shape[0]
    got = got_ref[0:states, :].astype(F32)
    if from_message:
        pieces = got_ref[states : states + 16, :].astype(F32)
        other = pieces[0:1] + pieces[1:2] + pieces[2:3]
    else:
        other = other_ref[0:1, :]
    mine = tot_ref[0:1, :]
    first = place_in_pair() == first_is
    later = jnp.exp2(jnp.where(first, other, mine))
    keep = keep_ref[...]
    both = jnp.where(first, later * keep + got, later * got + keep)
    both_ref[...] = both
    out_ref[0:states, :] = both.astype(BF16)
    out_ref[states : states + 16, :] = log_rows(jnp.broadcast_to(mine + other, (8, keep.shape[1])))
    other_out[...] = jnp.broadcast_to(other, other_out.shape)


def small_kernel(body, name, shapes, arrays, after):
    return pl.pallas_call(
        body,
        grid=(1,),
        in_specs=[pl.BlockSpec(a.shape, lambda i: (0, 0)) for a in arrays] + [token_ref(a) for a in after],
        out_specs=[pl.BlockSpec(shape, lambda i: (0, 0)) for shape, _ in shapes] + [token_ref()],
        out_shape=[jax.ShapeDtypeStruct(*s) for s in shapes] + [TOKEN],
        compiler_params=pltpu.CompilerParams(vmem_limit_bytes=4 * MIB),
        cost_estimate=pl.CostEstimate(flops=10**6, bytes_accessed=MIB, transcendentals=0),
        name=name,
    )(*arrays, *after)


def joined(keep, got, tot, other, up, after):
    states, half = keep.shape
    body = functools.partial(joined_kernel, first_is=0 if up else 1, from_message=other is None)
    shapes = [((states + 16, half), BF16), ((states, half), F32), ((8, half), F32)]
    return small_kernel(body, "joined", shapes, (keep, got, tot, tot if other is None else other), after)


def carry_kernel(both_ref, in_ref, tot_ref, other_ref, *refs, up):
    out_ref, token = refs[-2:]
    give(token)
    states = both_ref.shape[0]
    seen = (pairs_before(up) > 0).astype(F32)
    span = jnp.exp2(tot_ref[0:1, :] + other_ref[0:1, :]) * seen
    out_ref[...] = (both_ref[...] + span * in_ref[0:states, :].astype(F32)).astype(BF16)


def carry(both, into, tot, other, up, after):
    body = functools.partial(carry_kernel, up=up)
    return small_kernel(body, "carry", [(both.shape, BF16)], (both, into, tot, other), after)


def entered_kernel(keep_ref, got_ref, tot_ref, other_ref, near_ref, *refs, up, far):
    own_ref, partner_ref, token = refs[-3:]
    give(token)
    states = keep_ref.shape[0]
    enter = near_ref[0:states, :].astype(F32)
    if far:
        pieces = near_ref[states : states + 16, :].astype(F32)
        span = jnp.exp2(pieces[0:1] + pieces[1:2] + pieces[2:3])
        enter = enter + jnp.where(pairs_before(up) > 1, span * refs[0][...].astype(F32), 0.0)
    enter = jnp.where(pairs_before(up) > 0, enter, 0.0)
    mine, other = jnp.exp2(tot_ref[0:1, :]), jnp.exp2(other_ref[0:1, :])
    first = place_in_pair() == (0 if up else 1)
    after_me = mine * enter + keep_ref[...]
    after_other = other * enter + got_ref[0:states, :].astype(F32)
    own_ref[...] = jnp.where(first, enter, after_other).astype(BF16)
    partner_ref[...] = jnp.where(first, after_me, enter).astype(BF16)


def entered(keep, got, tot, other, near, far, up, after):
    body = functools.partial(entered_kernel, up=up, far=far is not None)
    shapes = [(keep.shape, BF16)] * 2
    arrays = (keep, got, tot, other, near) + (() if far is None else (far,))
    return small_kernel(body, "entered", shapes, arrays, after)


def hop(x, up, by, wrap):
    count = lax.axis_size("ctx")
    by = 2 * by if up else -2 * by
    return lax.ppermute(x, "ctx", [(i, (i + by) % count) for i in range(count) if wrap or 0 <= i + by < count])


def swap(x):
    return lax.ppermute(x, "ctx", [(i, i ^ 1) for i in range(lax.axis_size("ctx"))])


def reach(message, both, tot, other, up, after, wrap):
    count = lax.axis_size("ctx")
    near = hop(message, up, 1, wrap[0])
    if count == 8:
        out, token = carry(both, near, tot, other, up, after)
        return near, hop(out, up, 2, wrap[1]), token
    for _ in range(count // 2 - 2):
        out, token = carry(both, near, tot, other, up, after)
        near = hop(out, up, 1, wrap[0])
    return near, None, token


def block_diagonal(pair):
    low = low_lanes(pair.shape[0])
    wide = pair.astype(F32)
    zero = jnp.zeros_like(wide)
    return jnp.concatenate([jnp.where(low, wide, zero), jnp.where(low, zero, wide)], axis=0).astype(BF16)


def forward_kernel(x_ref, b_ref, c_ref, cum_ref, cumt_ref, after, y_ref, token, scores):
    rows = x_ref.shape[0]
    blocks = rows // BLOCK

    @pl.when(pl.program_id(0) == 0)
    def _():
        r = lax.broadcasted_iota(jnp.int32, (BLOCK, BLOCK), 0)
        c = lax.broadcasted_iota(jnp.int32, (BLOCK, BLOCK), 1)
        for k in range(blocks):
            at = slice(k * BLOCK, (k + 1) * BLOCK)
            scores[k] = jnp.where(r >= c, dot(c_ref[at, :], b_ref[at, :], NT), 0.0)

    low = low_lanes(BLOCK)
    b_t = [transposed(b_ref[k * BLOCK : (k + 1) * BLOCK, :]) for k in range(blocks)]
    for p in range(GROUP_HEADS // 2):
        ps = slice(p * LANES, (p + 1) * LANES)
        state = None
        for k in range(blocks):
            at = slice(k * BLOCK, (k + 1) * BLOCK)
            a0 = jnp.broadcast_to(cum_ref[0, at, 2 * p : 2 * p + 1], (BLOCK, LANES))
            a1 = jnp.broadcast_to(cum_ref[0, at, 2 * p + 1 : 2 * p + 2], (BLOCK, LANES))
            r0 = cumt_ref[2 * p : 2 * p + 1, at]
            r1 = cumt_ref[2 * p + 1 : 2 * p + 2, at]
            s = scores[k]
            w0 = jnp.exp2(jnp.minimum(a0 - r0, 0.0)) * s
            w1 = jnp.exp2(jnp.minimum(a1 - r1, 0.0)) * s
            x = x_ref[at, ps]
            y = dot(jnp.concatenate([w0, w1], axis=1).astype(BF16), block_diagonal(x))
            both = jnp.where(low, a0, a1)
            if k > 0:
                y = y + jnp.exp2(both) * dot(c_ref[at, :], state.astype(BF16))
            if k < blocks - 1:
                last = both[BLOCK - 1 :, :]
                fresh = dot(b_t[k], (x.astype(F32) * jnp.exp2(last - both)).astype(BF16))
                state = fresh if k == 0 else jnp.exp2(last) * state + fresh
            y_ref[at, ps] = y
    give(token)


def forward(x, b, c, cum, cumt, first, groups, after):
    rows = x.shape[0]
    wide = x.shape[1] // cum.shape[0]
    return pl.pallas_call(
        forward_kernel,
        grid=(groups,),
        in_specs=[
            pl.BlockSpec((rows, wide), lambda g: (0, first + g)),
            pl.BlockSpec(b.shape, lambda g: (0, 0)),
            pl.BlockSpec(c.shape, lambda g: (0, 0)),
            pl.BlockSpec((1, rows, GROUP_HEADS), lambda g: (first + g, 0, 0)),
            pl.BlockSpec((GROUP_HEADS, rows), lambda g: (first + g, 0)),
            token_ref(),
        ],
        out_specs=[pl.BlockSpec((rows, wide), lambda g: (0, g)), token_ref()],
        out_shape=[jax.ShapeDtypeStruct((rows, wide * groups), F32), TOKEN],
        scratch_shapes=[pltpu.VMEM((rows // BLOCK, BLOCK, BLOCK), F32)],
        compiler_params=pltpu.CompilerParams(vmem_limit_bytes=8 * MIB),
        cost_estimate=pl.CostEstimate(flops=3 * 10**9, bytes_accessed=4 * MIB, transcendentals=3 * 10**6),
        name="forward",
    )(x, b, c, cum, cumt, after)


def finish_kernel(y_ref, c_ref, lead_ref, own_ref, back_ref, after, out_ref, state_ref, token, *, half):
    state = jnp.where(half == place_in_pair(), own_ref[...].astype(F32), back_ref[...].astype(F32)).astype(BF16)
    state_ref[...] = state
    give(token)
    for p in range(GROUP_HEADS // 2):
        ps = slice(p * LANES, (p + 1) * LANES)
        lead = pair_columns(lead_ref[0], p)
        out_ref[:, ps] = (y_ref[:, ps] + lead * dot(c_ref[...], state[:, ps])).astype(BF16)


def finish(y, c, lead, own, back, half, after):
    rows, width = y.shape
    states = own.shape[0]
    wide = width // 2
    first = 2 * half
    return pl.pallas_call(
        functools.partial(finish_kernel, half=half),
        grid=(2,),
        in_specs=[
            pl.BlockSpec((rows, wide), lambda g: (0, g)),
            pl.BlockSpec(c.shape, lambda g: (0, 0)),
            pl.BlockSpec((1, rows, GROUP_HEADS), lambda g: (first + g, 0, 0)),
            pl.BlockSpec((states, wide), lambda g: (0, g)),
            pl.BlockSpec((states, wide), lambda g: (0, g)),
            token_ref(),
        ],
        out_specs=[pl.BlockSpec((rows, wide), lambda g: (0, g)), pl.BlockSpec((states, wide), lambda g: (0, g)), token_ref()],
        out_shape=[jax.ShapeDtypeStruct((rows, width), BF16), jax.ShapeDtypeStruct((states, width), BF16), TOKEN],
        compiler_params=pltpu.CompilerParams(vmem_limit_bytes=8 * MIB),
        cost_estimate=pl.CostEstimate(flops=3 * 10**8, bytes_accessed=4 * MIB, transcendentals=0),
        name="finish",
    )(y, c, lead, own, back, after)


def adjoint_kernel(dout_ref, w_ref, c_ref, lead_ref, after, *refs, group):
    gy_ref, keep_ref, send_ref, token = refs[-4:]
    c_t = transposed(c_ref[...])
    gy = dot(dout_ref[...], w_ref[...])
    gy_ref[...] = gy.astype(BF16)
    give(token)
    mine = group == place_in_pair()
    for p in range(GROUP_HEADS // 2):
        ps = slice(p * LANES, (p + 1) * LANES)
        scaled = gy[:, ps] * pair_columns(lead_ref[0], p)
        own = dot(c_t, scaled.astype(BF16))
        if group == 0:
            keep_ref[:, ps] = own
            send_ref[:, ps] = own.astype(BF16)
        else:
            keep_ref[:, ps] = jnp.where(mine, own, refs[0][:, ps])
            send_ref[:, ps] = jnp.where(mine, refs[1][:, ps].astype(F32), own).astype(BF16)


def adjoint(dout, w, c, lead, group, after, before):
    rows, model = dout.shape
    wide = w.shape[1] // lead.shape[0]
    first = 2 * group
    states = c.shape[1]
    state = pl.BlockSpec((states, wide), lambda g: (0, g))
    return pl.pallas_call(
        functools.partial(adjoint_kernel, group=group),
        grid=(2,),
        in_specs=[
            pl.BlockSpec((rows, model), lambda g: (0, 0)),
            pl.BlockSpec((model, wide), lambda g: (0, first + g)),
            pl.BlockSpec(c.shape, lambda g: (0, 0)),
            pl.BlockSpec((1, rows, GROUP_HEADS), lambda g: (first + g, 0, 0)),
            token_ref(),
        ] + [state] * len(before),
        out_specs=[pl.BlockSpec((rows, wide), lambda g: (0, g)), state, state, token_ref()],
        out_shape=[
            jax.ShapeDtypeStruct((rows, 2 * wide), BF16),
            jax.ShapeDtypeStruct((states, 2 * wide), F32),
            jax.ShapeDtypeStruct((states, 2 * wide), BF16),
            TOKEN,
        ],
        compiler_params=pltpu.CompilerParams(vmem_limit_bytes=16 * MIB),
        cost_estimate=pl.CostEstimate(flops=3 * 10**9, bytes_accessed=8 * MIB, transcendentals=0),
        name="adjoint",
    )(dout, w, c, lead, after, *before)


def turn_kernel(dout_ref, after, out_ref, token, *, ring):
    count = len(ring)
    tall = dout_ref.shape[1] // count
    me = lax.axis_index("ctx")
    give(token)
    for i in range(count):
        to = sum(jnp.where(me == ring[j], ring[(j + i) % count], 0) for j in range(count))
        block = dout_ref[:, pl.ds(pl.multiple_of(to * tall, LANES), tall)]
        out_ref[i * tall : (i + 1) * tall, :] = transposed(block)


def turn(dout, ring, after):
    rows, model = dout.shape
    return pl.pallas_call(
        functools.partial(turn_kernel, ring=ring),
        grid=(1,),
        in_specs=[pl.BlockSpec(dout.shape, lambda i: (0, 0)), token_ref()],
        out_specs=[pl.BlockSpec((model, rows), lambda i: (0, 0)), token_ref()],
        out_shape=[jax.ShapeDtypeStruct((model, rows), BF16), TOKEN],
        compiler_params=pltpu.CompilerParams(vmem_limit_bytes=12 * MIB),
        cost_estimate=pl.CostEstimate(flops=0, bytes_accessed=4 * MIB, transcendentals=0),
        name="turn",
    )(dout, after)


def backward_kernel(
    x_ref, gy_ref, y_ref, b_ref, c_ref, cum_ref, cumt_ref, s_ref, own_ref, back_ref, after,
    *refs, group, more,
):
    gx_ref, db_ref, dc_ref, dl_ref, scores, dscores = refs[-6:]
    rows = x_ref.shape[0]
    blocks = rows // BLOCK
    step, steps = pl.program_id(0), pl.num_programs(0)
    r = lax.broadcasted_iota(jnp.int32, (BLOCK, BLOCK), 0)
    c = lax.broadcasted_iota(jnp.int32, (BLOCK, BLOCK), 1)
    upper = r <= c

    @pl.when(step == 0)
    def _():
        for k in range(blocks):
            at = slice(k * BLOCK, (k + 1) * BLOCK)
            scores[k] = jnp.where(upper, dot(b_ref[at, :], c_ref[at, :], NT), 0.0)
        dscores[...] = jnp.zeros_like(dscores)
        db_ref[...] = refs[1][...] if more else jnp.zeros_like(db_ref)
        dc_ref[...] = refs[2][...] if more else jnp.zeros_like(dc_ref)

    low = low_lanes(BLOCK)
    leaving = jnp.where(group == place_in_pair(), own_ref[...].astype(F32), back_ref[...].astype(F32))
    spots = [slice(k * BLOCK, (k + 1) * BLOCK) for k in range(blocks)]
    b_t = [transposed(b_ref[at, :]) for at in spots]
    c_t = [transposed(c_ref[at, :]) for at in spots]
    sums = [jnp.zeros((GROUP_HEADS, BLOCK), F32)] * blocks
    head_row = lax.broadcasted_iota(jnp.int32, (GROUP_HEADS, LANES), 0)
    head_half = lax.broadcasted_iota(jnp.int32, (GROUP_HEADS, LANES), 1) // (LANES // 2)
    for p in range(GROUP_HEADS // 2):
        ps = slice(p * LANES, (p + 1) * LANES)
        place = (head_row == 2 * p + head_half).astype(BF16)
        columns, tails, entering = [], [], [s_ref[:, ps].astype(F32)]
        for k, at in enumerate(spots):
            a0 = jnp.broadcast_to(cum_ref[0, at, 2 * p : 2 * p + 1], (BLOCK, LANES))
            a1 = jnp.broadcast_to(cum_ref[0, at, 2 * p + 1 : 2 * p + 2], (BLOCK, LANES))
            both = jnp.where(low, a0, a1)
            last = both[BLOCK - 1 :, :]
            columns.append((a0, a1, both, jnp.exp2(last)))
            tail = jnp.exp2(last - both)
            tails.append((tail, (x_ref[at, ps].astype(F32) * tail).astype(BF16)))
            entering.append(jnp.exp2(last) * entering[k] + dot(b_t[k], tails[k][1]))
        g = leaving[:, ps]
        for k in reversed(range(blocks)):
            at = spots[k]
            a0, a1, both, span = columns[k]
            tail, xs = tails[k]
            d0 = jnp.exp2(jnp.minimum(cumt_ref[2 * p : 2 * p + 1, at] - a0, 0.0))
            d1 = jnp.exp2(jnp.minimum(cumt_ref[2 * p + 1 : 2 * p + 2, at] - a1, 0.0))
            s = scores[k]
            x, gy = x_ref[at, ps], gy_ref[at, ps]
            g_half = g.astype(BF16)
            weights = jnp.concatenate([d0 * s, d1 * s], axis=1).astype(BF16)
            gx = dot(weights, block_diagonal(gy)) + tail * dot(b_ref[at, :], g_half)
            gx_ref[at, ps] = gx.astype(BF16)
            dw = dot(block_diagonal(x), gy, NT)
            dscores[k] += d0 * dw[:BLOCK] + d1 * dw[BLOCK:]
            db_ref[at, :] += dot(xs, g_half, NT)
            gys = (gy.astype(F32) * jnp.exp2(both)).astype(BF16)
            dc_ref[at, :] += dot(gys, entering[k].astype(BF16), NT)
            term = gy.astype(F32) * y_ref[at, ps].astype(F32) - x.astype(F32) * gx
            end = jnp.sum(entering[k + 1] * g, axis=0, keepdims=True)
            term = term + jnp.where(r == BLOCK - 1, end, 0.0)
            hi = term.astype(BF16)
            lo = (term - hi.astype(F32)).astype(BF16)
            sums[k] = sums[k] + dot(place, hi, NT) + dot(place, lo, NT)
            g = span * g + dot(c_t[k], gys)
    for k, at in enumerate(spots):
        dl_ref[:, at] = dot(sums[k], (r >= c).astype(F32), precision=EXACT)

    @pl.when(step == steps - 1)
    def _():
        for k, at in enumerate(spots):
            ds = jnp.where(upper, dscores[k], 0.0)
            db_ref[at, :] += dot(ds.astype(BF16), c_ref[at, :])
            dc_ref[at, :] += dot(ds.T.astype(BF16), b_ref[at, :])


def backward(x, gy, y, b, c, cum, cumt, entering, own, back, group, half, after, grads):
    rows, width = x.shape
    states = own.shape[0]
    wide = own.shape[1] // 2
    spot = 2 * group + half
    heads = GROUP_HEADS * cum.shape[0]
    here = pl.BlockSpec((rows, wide), lambda g: (0, half))
    whole = pl.BlockSpec((rows, states), lambda g: (0, 0))
    left = pl.BlockSpec(memory_space=pl.ANY)
    return pl.pallas_call(
        functools.partial(backward_kernel, group=group, more=bool(grads)),
        grid=(1,),
        in_specs=[
            pl.BlockSpec((rows, wide), lambda g: (0, spot)),
            here, here, whole, whole,
            pl.BlockSpec((1, rows, GROUP_HEADS), lambda g: (spot, 0, 0)),
            pl.BlockSpec((GROUP_HEADS, rows), lambda g: (spot, 0)),
            pl.BlockSpec((states, wide), lambda g: (0, half)),
            pl.BlockSpec((states, wide), lambda g: (0, half)),
            pl.BlockSpec((states, wide), lambda g: (0, half)),
            token_ref(after),
        ] + ([left, whole, whole, left] if grads else []),
        out_specs=[
            pl.BlockSpec((rows, wide), lambda g: (0, spot)),
            whole, whole, pl.BlockSpec((GROUP_HEADS, rows), lambda g: (spot, 0)),
        ],
        out_shape=[
            jax.ShapeDtypeStruct((rows, width), BF16),
            jax.ShapeDtypeStruct((rows, states), F32),
            jax.ShapeDtypeStruct((rows, states), F32),
            jax.ShapeDtypeStruct((heads, rows), F32),
        ],
        scratch_shapes=[pltpu.VMEM((rows // BLOCK, BLOCK, BLOCK), F32)] * 2,
        input_output_aliases={11: 0, 14: 3} if grads else {},
        compiler_params=pltpu.CompilerParams(vmem_limit_bytes=14 * MIB),
        cost_estimate=pl.CostEstimate(flops=3 * 10**9, bytes_accessed=3 * MIB, transcendentals=10**6),
        name="backward",
    )(x, gy, y, b, c, cum, cumt, entering, own, back, after, *grads)


def close_kernel(dout_ref, y_ref, got_ref, *refs):
    refs[-1][...] = dot(dout_ref[...], y_ref[...]) + got_ref[...].astype(F32)


def close(dout_t, y, got, flow, flows, before):
    tall, wide = got.shape
    rows = dout_t.shape[1]
    return pl.pallas_call(
        close_kernel,
        grid=(1,),
        in_specs=[
            pl.BlockSpec((tall, rows), lambda i: (0, 0)),
            pl.BlockSpec((rows, wide), lambda i: (0, flow % 2)),
            pl.BlockSpec((tall, wide), lambda i: (0, 0)),
        ] + [pl.BlockSpec(memory_space=pl.ANY)] * len(before),
        out_specs=pl.BlockSpec((tall, wide), lambda i: (0, flow)),
        out_shape=jax.ShapeDtypeStruct((tall, wide * flows), F32),
        input_output_aliases={3: 0} if before else {},
        compiler_params=pltpu.CompilerParams(vmem_limit_bytes=6 * MIB),
        cost_estimate=pl.CostEstimate(flops=2 * 10**8, bytes_accessed=MIB, transcendentals=0),
        name="close",
    )(dout_t, y, got, *before)


def ring_order(count):
    if count == 8:
        return [0, 2, 4, 6, 7, 5, 3, 1]
    return list(range(count))


def on_device(x, b, c, loga, dout, w):
    count = lax.axis_size("ctx")
    rows, width = x.shape
    wide = width // 2
    eighth = 2
    ring = ring_order(count)
    tall = dout.shape[1] // count

    cum, cumt, lead, keep, tot, send = start(loga.T, x, b)
    got = swap(send)
    gy0, *ends, token = adjoint(dout, w, c, lead, 0, tot, ())
    message, both, other, token = joined(keep, got, tot, None, True, (token,))
    gy1, keep_b, send_b, token = adjoint(dout, w, c, lead, 1, token, ends)
    gys = (gy0, gy1)
    near, far, token = reach(message, both, tot, other, True, (token,), (True, False))
    got_b = swap(send_b)
    y0, token = forward(x, b, c, cum, cumt, 0, eighth, token)
    message_b, both_b, _, token = joined(keep_b, got_b, tot, other, False, (token,))
    y1, token = forward(x, b, c, cum, cumt, eighth, eighth, token)
    dout_t, token = turn(dout, ring, token)
    own, partners, token = entered(keep, got, tot, other, near, far, True, (token,))
    back = swap(partners)
    near_b, far_b, token = reach(message_b, both_b, tot, other, False, (token,), (False, True))
    y_half, entering = [], []
    for g, y in enumerate((y0, y1)):
        y, state, token = finish(y, c, lead, own, back, g, token)
        y_half.append(y)
        entering.append(state)

    flows = []
    for g in range(2):
        for f, by in enumerate((1, -1)):
            hops = [(ring[i], ring[(i + by) % count]) for i in range(count)]
            flows.append([hops, by, y_half[g][:, f * wide // 2 : (f + 1) * wide // 2], None])
    passed = []
    for step in range(count - 1):
        for flow in flows:
            hops, by, y, got_sum = flow
            offset = (by * (count - 1 - step)) % count
            part = dot(dout_t[offset * tall : (offset + 1) * tall], y)
            if got_sum is not None:
                part = part + got_sum.astype(F32)
            flow[3] = lax.ppermute(part.astype(BF16), "ctx", hops)
        passed.append([flow[3] for flow in flows])
    before = ()
    for f, flow in enumerate(flows):
        before = (close(dout_t, y_half[f // 2], flow[3], f, len(flows), before),)
    weight_grad = before[0]

    own_b, partners_b, _ = entered(keep_b, got_b, tot, other, near_b, far_b, False, (passed[0][2],))
    back_b = swap(partners_b)
    grads = ()
    late = ((1, 2), (2, 2), (3, 2), (4, 2))
    for g in range(2):
        for h in range(2):
            step, f = late[2 * g + h]
            grads = backward(x, gys[g], y_half[g], b, c, cum, cumt, entering[g], own_b, back_b, g, h, passed[step][f], grads)
    grad_x, db, dc, dl = grads
    terms = jnp.concatenate([db, dc], axis=0).astype(BF16)
    summed = terms.astype(F32) + lax.ppermute(terms, "head", [(0, 1), (1, 0)]).astype(F32)
    return grad_x, summed[:rows], summed[rows:], dl.T, weight_grad


def solution(mesh):
    tokens = ("group", "ctx")
    placed = (
        P(tokens, "head"),
        P(tokens, None),
        P(tokens, None),
        P(tokens, "head"),
        P(tokens, None),
        P(None, "head"),
    )
    return jax.shard_map(
        on_device,
        mesh=mesh,
        in_specs=placed,
        out_specs=(
            P(tokens, "head"),
            P(tokens, None),
            P(tokens, None),
            P(tokens, "head"),
            P(tokens, "head"),
        ),
        check_vma=False,
    )
```
